32 devices in a mesh: head: 4 (over y, core), tail: 8 (over z, x).
Axes of the slice: x: 2, y: 2, z: 4, core: 2. Of those that a mesh axis runs over, the one named last changes fastest.
Arguments:
- head_table: float32 [16384, 512], P(('head', 'tail')), may hold values from -2.5 to 2.5
- head_state: float32 [16384], P(('head', 'tail')), may hold values from 0.01 to 0.1
- tail_table: float32 [16384, 512], P(('head', 'tail')), may hold values from -2.5 to 2.5
- tail_state: float32 [16384], P(('head', 'tail')), may hold values from 0.01 to 0.1
- relations: float32 [1024, 512], P(('head', 'tail')), may hold values from -0.25 to 0.25
- relation_state: float32 [1024, 512], P(('head', 'tail')), may hold values from 10 to 100
- head_rows: int32 [2, 16384], P(None, ('head', 'tail')), may hold values from 0 to 511
- tail_rows: int32 [2, 16384], P(None, ('head', 'tail')), may hold values from 0 to 511
- negatives: int32 [2, 128, 128], P(None, ('head', 'tail')), may hold values from 0 to 511
- relation_ids: int32 [2, 128], P(None, ('head', 'tail')), may hold values from 0 to 1
- block_counts: int32 [2, 32], P(None, ('head', 'tail')), may hold values from 1 to 4, 64 in all within a row
Outputs:
- heads_out: float32 [16384, 512], P(('head', 'tail'))
- tails_out: float32 [16384, 512], P(('head', 'tail'))
- relations_out: float32 [1024, 512], P(('head', 'tail'))
The draws below stay inside these ranges and needn't reach their ends.
Inputs may be any that keep to these rules, and one draw needn't show every extreme that they name: `block_counts`: in each bucket the counts over all devices sum to 4 // 2 times the number of devices, and some device has 4.
All inputs are finite; a program needn't handle non-finite values.
Results may differ from the reference program's by a relative error of at most 0.01.
Values may be sent and summed in bfloat16 or wider, within the bound.
No kernel may reach another device: no remote copies, remote signals or barrier semaphores. Data moves between devices by JAX's collectives and lax.ppermute only.
A program may use at most 64 MiB of HBM per device.

```python
import math
import jax
import jax.numpy as jnp
import numpy as np
from jax import lax

D = 512
NREL = 2
BLOCK = 128
NNEG = 128
EB = 4
HROWS = 512
TROWS = 512
HEAD_ENTITIES = 16384
TAIL_ENTITIES = 16384
EDGE_SLOTS = 16384
EDGE_BLOCKS = 128
N_HEAD = 4
N_TAIL = 8
DEVICES = 32


def plant(result, key, low, high):
    spot = [jax.random.randint(jax.random.fold_in(key, axis), (), 0, length) for axis, length in enumerate(result.shape)]
    longest = result.shape.index(max(result.shape))
    neighbour = spot[:longest] + [(spot[longest] + 1) % result.shape[longest]] + spot[longest + 1:]
    return result.at[tuple(spot)].set(low).at[tuple(neighbour)].set(high)


def block_levels(stream_key, extent, cuts, low, largest):
    def one(axis_at, shards_of):
        heights = jax.random.uniform(jax.random.fold_in(jax.random.fold_in(stream_key, 6), axis_at), (shards_of,), jnp.float32, low / len(cuts), largest / len(cuts))
        return jnp.repeat(jnp.exp(heights), extent[axis_at] // shards_of).reshape((-1,) + (1,) * (len(extent) - axis_at - 1))

    factor_of = one(*cuts[0])
    for cut in cuts[1:]:
        factor_of = factor_of * one(*cut)
    return factor_of


def length_profile(count, total, reach, lean):
    loads = [(1 << 20) // math.isqrt(rank ** lean) + 1 for rank in range(2, count + 1)]
    surplus, given = total - reach - (count - 1), [1] * (count - 1)
    while surplus > 0:
        free = [i for i in range(count - 1) if given[i] < reach]
        mass, remaining = sum([loads[i] for i in free]), surplus
        for i in free:
            extra = min(reach - given[i], max(1, remaining * loads[i] // mass), surplus)
            given[i] = given[i] + extra
            surplus = surplus - extra
    return np.array([reach] + given)


def ragged_sizes(rng, amount, total, bound, slope):
    if amount == 2:
        one = jax.random.randint(rng, (), max(1, total - bound), min(bound, total - 1) + 1)
        return jnp.stack([one, total - one])
    lengths = jnp.asarray(length_profile(amount, total, bound, slope), jnp.int32)
    pairs = (amount - 1) // 2
    donor, taker = lengths[1:1 + 2 * pairs:2], lengths[2:2 + 2 * pairs:2]
    margin = jnp.minimum(donor - 1, bound - taker)
    passed = jax.random.randint(jax.random.fold_in(rng, 1), (pairs,), 0, 1 << 20) % (margin + 1)
    lengths = lengths.at[1:1 + 2 * pairs:2].set(donor - passed).at[2:2 + 2 * pairs:2].set(taker + passed)
    return lengths[jax.random.permutation(jax.random.fold_in(rng, 2), amount)]


def noise(rng, extent, width, limit, cuts=(), kind=jnp.bfloat16):
    drawn = jax.random.normal(rng, extent, jnp.float32) * width
    if len(cuts) > 0:
        drawn = block_levels(rng, extent, cuts, -0.22, 0.18) * drawn
    return jnp.clip(drawn, min=-limit, max=limit).astype(kind)


def setup_inputs(seed: int = 0) -> dict:
    key_list = jax.random.split(jax.random.key(seed), 12)
    return {
        "head_table": noise(key_list[0], (HEAD_ENTITIES, D), 0.3, 2.5, ((0, 32),), jnp.float32),
        "head_state": jnp.clip(jnp.exp(math.log(0.1) - 2.3025851 * jax.random.uniform(key_list[1], (HEAD_ENTITIES,), jnp.float32) ** block_levels(key_list[1], (HEAD_ENTITIES,), ((0, 32),), -0.2, 0.2)), 0.01, 0.1),
        "tail_table": noise(key_list[2], (TAIL_ENTITIES, D), 0.3, 2.5, ((0, 32),), jnp.float32),
        "tail_state": jnp.clip(jnp.exp(math.log(0.1) - 2.3025851 * jax.random.uniform(key_list[3], (TAIL_ENTITIES,), jnp.float32) ** block_levels(key_list[3], (TAIL_ENTITIES,), ((0, 32),), -0.2, 0.2)), 0.01, 0.1),
        "relations": noise(key_list[4], (NREL * D, D), D ** -0.5, 0.25, ((0, 32),), jnp.float32),
        "relation_state": jnp.clip(jnp.exp(math.log(100.0) - 2.3025851 * jax.random.uniform(key_list[5], (NREL * D, D), jnp.float32) ** block_levels(key_list[5], (NREL * D, D), ((0, 32),), -0.2, 0.2)), 10.0, 100.0),
        "head_rows": plant(jax.random.randint(key_list[6], (2, EDGE_SLOTS), 0, HROWS), jax.random.fold_in(key_list[6], 1), 0, HROWS - 1).astype(jnp.int32),
        "tail_rows": plant(jax.random.randint(key_list[7], (2, EDGE_SLOTS), 0, TROWS), jax.random.fold_in(key_list[7], 1), 0, TROWS - 1).astype(jnp.int32),
        "negatives": plant(jax.random.randint(key_list[8], (2, EDGE_BLOCKS, NNEG), 0, TROWS), jax.random.fold_in(key_list[8], 1), 0, TROWS - 1).astype(jnp.int32),
        "relation_ids": plant(jax.random.randint(key_list[9], (2, EDGE_BLOCKS), 0, NREL), jax.random.fold_in(key_list[9], 1), 0, NREL - 1).astype(jnp.int32),
        "block_counts": jax.vmap(lambda own: ragged_sizes(own, DEVICES, (EB // 2) * DEVICES, EB, 2))(jax.random.split(key_list[10], 2)).reshape((2, DEVICES)).astype(jnp.int32),
    }


RATE_ROWS = 0.2
RATE_RELATIONS = 0.05
EPSILON = 1e-06

def row_adagrad(emb_table, row_state, gradient):
    state_new = row_state + lax.optimization_barrier(jnp.mean(gradient * gradient, axis=1))
    table_new = emb_table - RATE_ROWS * gradient / (jnp.sqrt(state_new) + EPSILON)[:, None]
    return (table_new, state_new)

def relation_adagrad(rel_table, rel_state, gradient):
    state_new = rel_state + gradient * gradient
    return (rel_table - RATE_RELATIONS * gradient / (jnp.sqrt(state_new) + EPSILON), state_new)

def score_bucket(head_table, head_state, tail_table, tail_state, rel_bf, head_index, tail_index, neg_index, rel_index, live_blocks):
    model_width = head_table.shape[1]
    block_total = rel_index.shape[0]
    per_block = head_index.shape[0] // block_total
    neg_total = neg_index.shape[1]
    rel_total = rel_bf.shape[0] // model_width
    head_vecs = head_table[head_index].astype(jnp.bfloat16).reshape(block_total, per_block, model_width)
    tail_vecs = tail_table[tail_index].astype(jnp.bfloat16).reshape(block_total, per_block, model_width)
    neg_vecs = tail_table[neg_index].astype(jnp.bfloat16)
    chosen = rel_bf.reshape(rel_total, model_width, model_width)[rel_index]
    live_mask = (jnp.arange(block_total, dtype=jnp.int32) < live_blocks).astype(jnp.float32)
    chosen_wide = chosen.astype(jnp.float32)
    projected = jnp.einsum('bed,bdk->bek', head_vecs.astype(jnp.float32), chosen_wide).astype(jnp.bfloat16)
    proj_wide = projected.astype(jnp.float32)
    tail_wide = tail_vecs.astype(jnp.float32)
    neg_wide = neg_vecs.astype(jnp.float32)
    pos_score = jnp.einsum('bek,bek->be', proj_wide, tail_wide)
    neg_score = jnp.einsum('bek,bnk->ben', proj_wide, neg_wide)
    pos_weight = -jax.nn.sigmoid(-pos_score) * live_mask[:, None]
    neg_weight = (jax.nn.sigmoid(neg_score) * live_mask[:, None, None] / neg_total).astype(jnp.bfloat16)
    neg_weight_wide = neg_weight.astype(jnp.float32)
    edge_grad = (pos_weight[:, :, None] * tail_wide + jnp.einsum('ben,bnk->bek', neg_weight_wide, neg_wide)).astype(jnp.bfloat16)
    head_terms = jnp.einsum('bek,bdk->bed', edge_grad.astype(jnp.float32), chosen_wide).reshape(-1, model_width)
    head_grad = jnp.zeros(head_table.shape, jnp.float32).at[head_index].add(head_terms)
    pos_terms = (pos_weight[:, :, None] * proj_wide).reshape(-1, model_width)
    neg_terms = jnp.einsum('ben,bek->bnk', neg_weight_wide, proj_wide).reshape(-1, model_width)
    tail_grad = jnp.zeros(tail_table.shape, jnp.float32).at[tail_index].add(pos_terms)
    tail_grad = tail_grad.at[neg_index.reshape(-1)].add(neg_terms)
    head_new, head_state_new = row_adagrad(head_table, head_state, head_grad)
    tail_new, tail_state_new = row_adagrad(tail_table, tail_state, tail_grad)
    onehot = (rel_index[:, None] == jnp.arange(rel_total, dtype=jnp.int32)[None, :]).astype(jnp.bfloat16)
    spread = (head_vecs[:, :, None, :] * onehot[:, None, :, None]).reshape(-1, rel_total * model_width)
    grad_term = jnp.dot(spread.T, edge_grad.reshape(-1, model_width), preferred_element_type=jnp.float32)
    return (head_new, head_state_new, tail_new, tail_state_new, grad_term)

def run_bucket(rel_bf, head_table, head_state, tail_table, tail_state, head_index, tail_index, neg_index, rel_index, live_blocks):

    def per_device(grad_sum, pieces):
        results = score_bucket(pieces[0], pieces[1], pieces[2], pieces[3], rel_bf, pieces[4], pieces[5], pieces[6], pieces[7], pieces[8])
        return (grad_sum + results[4], (results[0], results[1], results[2], results[3]))
    zero_sum = jnp.zeros((rel_bf.shape[0], rel_bf.shape[1]), jnp.float32)
    grad_sum, blocks = lax.scan(per_device, zero_sum, (head_table, head_state, tail_table, tail_state, head_index, tail_index, neg_index, rel_index, live_blocks))
    return (grad_sum, blocks)

def reference(head_table, head_state, tail_table, tail_state, relations, relation_state, head_rows, tail_rows, negatives, relation_ids, block_counts):
    devices_all = N_HEAD * N_TAIL
    slots = EB * BLOCK
    head_blocks = head_table.reshape(devices_all, HROWS, D)
    head_states = head_state.reshape(devices_all, HROWS)
    tail_blocks = tail_table.reshape(devices_all, TROWS, D)
    tail_states = tail_state.reshape(devices_all, TROWS)
    rel_table = relations
    rel_state = relation_state
    for bucket in range(2):
        if bucket == 1:
            tail_blocks = jnp.roll(tail_blocks.reshape(N_HEAD, N_TAIL, TROWS, D), 1, axis=1).reshape(devices_all, TROWS, D)
            tail_states = jnp.roll(tail_states.reshape(N_HEAD, N_TAIL, TROWS), 1, axis=1).reshape(devices_all, TROWS)
        rel_bf = rel_table.astype(jnp.bfloat16)
        grad_sum, blocks = run_bucket(rel_bf, head_blocks, head_states, tail_blocks, tail_states, head_rows[bucket].reshape(devices_all, slots), tail_rows[bucket].reshape(devices_all, slots), negatives[bucket].reshape(devices_all, EB, NNEG), relation_ids[bucket].reshape(devices_all, EB), block_counts[bucket])
        head_blocks, head_states, tail_blocks, tail_states = blocks
        rel_table, rel_state = relation_adagrad(rel_table, rel_state, grad_sum)
    return (head_blocks.reshape(-1, D), tail_blocks.reshape(-1, D), rel_table)
```

```python
import functools

import jax
import jax.numpy as jnp
import numpy as np
from jax import lax
from jax.experimental import pallas as pl
from jax.experimental.pallas import tpu as pltpu
from jax.sharding import PartitionSpec as P

RATE_ROWS = 0.2
RATE_RELATIONS = 0.05
EPSILON = 1e-06
AXES = ("head", "tail")
F32, BF16 = jnp.float32, jnp.bfloat16
ROWS, COLS = 0, 1
PACK_ROWS = 16
VMEM_LIMIT = 24 * 1024 * 1024
VMEM = pl.BlockSpec(memory_space=pltpu.VMEM)
SMEM = pl.BlockSpec(memory_space=pltpu.SMEM)


def dot(a, b, contract_a, contract_b):
    return lax.dot_general(
        a, b, (((contract_a,), (contract_b,)), ((), ())), preferred_element_type=F32
    )


def to_column(row):
    return jnp.broadcast_to(row, (128, row.shape[1])).T


def spread(column, width):
    return jnp.concatenate([column] * (width // column.shape[1]), axis=1)


def adagrad_rows(table, state_row, gradient):
    width = gradient.shape[1]
    mean = jnp.sum(gradient * gradient, axis=1, keepdims=True) * (1.0 / width)
    state = to_column(state_row) + mean
    factor = RATE_ROWS / (jnp.sqrt(state) + EPSILON)
    return table - gradient * spread(factor, width), state


def one_hot_rows(index_row, rows):
    n = index_row.shape[1]
    return (lax.broadcasted_iota(jnp.int32, (rows, n), 0) == index_row).astype(F32).astype(BF16)


def by_relation(x, rel_ref, k, blocks, relation):
    size = x.shape[0] // blocks
    parts = []
    for b in range(blocks):
        part = x[b * size : (b + 1) * size]
        parts.append(jnp.where(rel_ref[k, b] == relation, part, jnp.zeros_like(part)))
    return jnp.concatenate(parts, axis=0)


def restore_relations(nat_ref, lo_ref, hi_ref, rel_s):
    half = lo_ref.shape[0]
    own = 2 * half // nat_ref.shape[0]
    if own % PACK_ROWS:
        rel_s[:half] = lo_ref[...]
        rel_s[half:] = hi_ref[...]
        return
    for part, ref in enumerate((lo_ref, hi_ref)):
        for j in range(half // own):
            block = nat_ref[part * (half // own) + j]
            rel_s[pl.ds(pl.multiple_of(block * own, own), own)] = ref[j * own : (j + 1) * own]


def prepare_kernel(
    head_ref, tail_ref, hrows_ref, trows_ref, neg_ref, h_ref, t_ref, tcol_ref, cnt_ref
):
    buckets = hrows_ref.shape[0]
    blocks, nneg = neg_ref.shape[1:]
    pick = one_hot_rows(hrows_ref[0:1, :], head_ref.shape[0])
    h_ref[...] = dot(pick, head_ref[...].astype(BF16), ROWS, ROWS).astype(BF16)
    t_ref[...] = tail_ref[...].astype(BF16)
    ones = jnp.ones((8, nneg), BF16)
    for k in range(buckets):
        tcol_ref[k] = to_column(trows_ref[k : k + 1, :].astype(F32))
        for b in range(blocks):
            hot = one_hot_rows(neg_ref[k, b : b + 1, :], tail_ref.shape[0])
            cnt_ref[k, b : b + 1, :] = dot(ones, hot, COLS, COLS)[0:1, :]


def score_kernel(
    k, nneg, nat_ref, live_ref, rel_ref, lo_ref, hi_ref, h_ref, t_ref, tcol_ref, cnt_ref,
    keep_ref, send_ref, w_ref, u_ref, gu_ref, rel_s, grad_s,
):
    edges, width = h_ref.shape
    blocks, rows = cnt_ref.shape[1:]
    size = edges // blocks
    relations = rel_s.shape[0] // width
    restore_relations(nat_ref, lo_ref, hi_ref, rel_s)
    masked = [by_relation(h_ref[...], rel_ref, k, blocks, r) for r in range(relations)]
    u = dot(masked[0], rel_s[0:width], COLS, ROWS)
    for r in range(1, relations):
        u = u + dot(masked[r], rel_s[r * width : (r + 1) * width], COLS, ROWS)
    u = u.astype(BF16)
    u_ref[...] = u
    tails = t_ref[0:rows]
    score = dot(u, tails, COLS, COLS)
    row_id = lax.broadcasted_iota(jnp.int32, (size, rows), 1).astype(F32)
    for b in range(blocks):
        part = slice(b * size, (b + 1) * size)
        live = jnp.where(live_ref[k, 0] > b, 1.0, 0.0)
        half_tanh = 0.5 * jnp.tanh(0.5 * score[part])
        negative = ((0.5 + half_tanh) * (live / nneg)).astype(BF16).astype(F32)
        positive = (0.5 - half_tanh) * live
        is_tail = spread(tcol_ref[k, part], rows) == row_id
        weight = cnt_ref[k, b : b + 1, :] * negative - jnp.where(is_tail, positive, 0.0)
        w_ref[part] = weight.astype(BF16)
    gu = dot(w_ref[...], tails, COLS, ROWS).astype(BF16)
    gu_ref[...] = gu
    for r in range(relations):
        grad_s[r * width : (r + 1) * width] = dot(masked[r], gu, ROWS, ROWS)
    half = keep_ref.shape[0]
    own = 2 * half // nat_ref.shape[0]
    if own % PACK_ROWS:
        keep_ref[...] = grad_s[:half].astype(BF16)
        send_ref[...] = grad_s[half:].astype(BF16)
        return
    for part, ref in enumerate((keep_ref, send_ref)):
        for j in range(half // own):
            block = nat_ref[part * (half // own) + j]
            rows_of = pl.ds(pl.multiple_of(block * own, own), own)
            ref[j * own : (j + 1) * own] = grad_s[rows_of].astype(BF16)


def tail_kernel(w_ref, u_ref, table_ref, state_ref, out_ref):
    rows, width = table_ref.shape
    gradient = dot(w_ref[...], u_ref[...], ROWS, ROWS)
    table, state = adagrad_rows(table_ref[...], state_ref[...], gradient)
    out_ref[0:rows] = table.astype(BF16)
    state_row = state.T[0:1, :]
    high = state_row.astype(BF16).astype(F32)
    row_id = lax.broadcasted_iota(jnp.int32, (PACK_ROWS, width), 0)
    packed = jnp.where(row_id == 0, high, jnp.where(row_id == 1, state_row - high, 0.0))
    out_ref[rows : rows + PACK_ROWS] = packed.astype(BF16)


def last_tail_kernel(w_ref, u_ref, packed_ref, out_ref):
    rows = out_ref.shape[0]
    gradient = dot(w_ref[...], u_ref[...], ROWS, ROWS)
    packed = packed_ref[rows : rows + PACK_ROWS].astype(F32)
    state_row = packed[0:1, :] + packed[1:2, :]
    out_ref[...] = adagrad_rows(packed_ref[0:rows].astype(F32), state_row, gradient)[0]


def head_kernel(
    k, blocks, nat_ref, rel_ref, lo_ref, hi_ref, gu_ref, hrows_ref, table_ref, state_ref, *rest
):
    out_ref, rel_s = rest[0], rest[-1]
    rows, width = table_ref.shape
    relations = rel_s.shape[0] // width
    restore_relations(nat_ref, lo_ref, hi_ref, rel_s)
    gu = gu_ref[...]
    terms = None
    for r in range(relations):
        part = by_relation(gu, rel_ref, k, blocks, r)
        term = dot(part, rel_s[r * width : (r + 1) * width], COLS, COLS)
        terms = term if terms is None else terms + term
    hot = one_hot_rows(hrows_ref[k : k + 1, :], rows)
    gradient = dot(hot, terms.astype(BF16), COLS, ROWS)
    table, state = adagrad_rows(table_ref[...], state_ref[...], gradient)
    out_ref[...] = table
    if len(rest) > 2:
        state_out_ref, h_ref = rest[1:3]
        state_out_ref[...] = state.T[0:1, :]
        pick = one_hot_rows(hrows_ref[k + 1 : k + 2, :], rows)
        h_ref[...] = dot(pick, table.astype(BF16), ROWS, ROWS).astype(BF16)


def call(kernel, outs, smem, scratch, flops, *args):
    outs = [jax.ShapeDtypeStruct(shape, kind) for shape, kind in outs]
    moved = sum(a.size * a.dtype.itemsize for a in (*args, *outs))
    return pl.pallas_call(
        kernel,
        out_shape=outs,
        in_specs=[SMEM] * smem + [VMEM] * (len(args) - smem),
        out_specs=[VMEM] * len(outs),
        scratch_shapes=scratch,
        compiler_params=pltpu.CompilerParams(vmem_limit_bytes=VMEM_LIMIT),
        cost_estimate=pl.CostEstimate(flops=flops, bytes_accessed=moved, transcendentals=0),
    )(*args)


class Exchange:
    def __init__(self, heads, tails):
        self.devices = heads * tails
        cores = [tails] if heads > 1 else []
        heads_left = [tails << i for i in range(1, heads.bit_length() - 1)]
        self.masks = cores + heads_left + [1 << i for i in range(tails.bit_length() - 1)]
        bits = len(self.masks)
        places = [
            sum(m for i, m in enumerate(self.masks) if j >> (bits - 1 - i) & 1)
            for j in range(self.devices)
        ]
        slots = np.zeros(self.devices, np.int32)
        slots[places] = np.arange(self.devices)
        me = lax.axis_index(AXES)
        self.block_of_slot = jnp.asarray(places, jnp.int32) ^ me
        self.slot_of_block = jnp.asarray(slots)[jnp.arange(self.devices, dtype=jnp.int32) ^ me]

    def swap(self, x, mask):
        return lax.ppermute(x, AXES, [(i, i ^ mask) for i in range(self.devices)])

    def reduce_scatter(self, keep, send):
        if (2 * keep.shape[0] // self.devices) % PACK_ROWS:
            both = jnp.concatenate([keep, send])
            both = both.reshape(self.devices, -1, both.shape[1])[self.block_of_slot]
            keep, send = jnp.split(both.reshape(-1, both.shape[2]), 2)
        for i, mask in enumerate(self.masks):
            got = self.swap(send, mask)
            half = keep.shape[0] // 2
            if i + 1 == len(self.masks):
                return keep.astype(F32) + got.astype(F32)
            send = (keep[half:].astype(F32) + got[half:].astype(F32)).astype(BF16)
            keep = (keep[:half].astype(F32) + got[:half].astype(F32)).astype(BF16)

    def all_gather(self, own):
        rows = own.shape[0]
        for mask in self.masks[:0:-1]:
            own = jnp.concatenate([own, self.swap(own, mask)])
        lo, hi = own, self.swap(own, self.masks[0])
        if rows % PACK_ROWS:
            both = jnp.concatenate([lo, hi]).reshape(self.devices, rows, -1)[self.slot_of_block]
            lo, hi = jnp.split(both.reshape(self.devices * rows, -1), 2)
        return lo, hi


def shards(
    head_table,
    head_state,
    tail_table,
    tail_state,
    relations,
    relation_state,
    head_rows,
    tail_rows,
    negatives,
    relation_ids,
    block_counts,
):
    heads, tails = lax.axis_size("head"), lax.axis_size("tail")
    exchange = Exchange(heads, tails)
    nat = exchange.block_of_slot
    rows, width = tail_table.shape
    edges = head_rows.shape[1]
    blocks, nneg = negatives.shape[1:]
    all_rows = relations.shape[0] * exchange.devices
    half = all_rows // 2
    square = 2 * rows * edges * width

    own_bf = relations.astype(BF16)
    head_vecs, tail_vecs, tail_col, counts = call(
        prepare_kernel,
        [
            ((edges, width), BF16),
            ((rows, width), BF16),
            ((2, edges, 128), F32),
            ((2, blocks, rows), F32),
        ],
        0, [], square,
        head_table, tail_table, head_rows, tail_rows, negatives,
    )
    head_state = head_state.reshape(1, -1)
    tail_state = tail_state.reshape(1, -1)
    for k in range(2):
        lo, hi = exchange.all_gather(own_bf)
        keep, send, weights, projected, edge_grad = call(
            functools.partial(score_kernel, k, float(nneg)),
            [
                ((half, width), BF16),
                ((half, width), BF16),
                ((edges, rows), BF16),
                ((edges, width), BF16),
                ((edges, width), BF16),
            ],
            3, [pltpu.VMEM((all_rows, width), BF16), pltpu.VMEM((all_rows, width), F32)], 6 * square,
            nat, block_counts, relation_ids, lo, hi, head_vecs, tail_vecs, tail_col, counts,
        )
        rel_scratch = [pltpu.VMEM((all_rows, width), BF16)]
        head_args = (nat, relation_ids, lo, hi, edge_grad, head_rows, head_table, head_state)
        if k == 0:
            (packed,) = call(
                tail_kernel, [((rows + PACK_ROWS, width), BF16)], 0, [], square,
                weights, projected, tail_table, tail_state,
            )
            tail_vecs = lax.ppermute(packed, "tail", [(i, (i + 1) % tails) for i in range(tails)])
            head_table, head_state, head_vecs = call(
                functools.partial(head_kernel, k, blocks),
                [(head_table.shape, F32), (head_state.shape, F32), ((edges, width), BF16)],
                2, rel_scratch, 4 * square, *head_args,
            )
        else:
            (tail_table,) = call(
                last_tail_kernel, [((rows, width), F32)], 0, [], square,
                weights, projected, tail_vecs,
            )
            (head_table,) = call(
                functools.partial(head_kernel, k, blocks), [(head_table.shape, F32)],
                2, rel_scratch, 3 * square, *head_args,
            )
        grad = exchange.reduce_scatter(keep, send)
        relation_state = relation_state + grad * grad
        relations = relations - RATE_RELATIONS * grad / (jnp.sqrt(relation_state) + EPSILON)
        own_bf = relations.astype(BF16)
    return (head_table, tail_table, relations)


def solution(mesh):
    both = P(AXES, None)
    in_specs = (
        both,
        P(AXES),
        both,
        P(AXES),
        both,
        both,
        P(None, AXES),
        P(None, AXES),
        P(None, AXES, None),
        P(None, AXES),
        P(None, AXES),
    )
    return jax.shard_map(
        shards, mesh=mesh, in_specs=in_specs, out_specs=(both, both, both), check_vma=False
    )
```

```python
import functools

import jax
import jax.numpy as jnp
import numpy as np
from jax import lax
from jax.experimental import pallas as pl
from jax.experimental.pallas import tpu as pltpu
from jax.sharding import PartitionSpec as P

RATE_ROWS = 0.2
RATE_RELATIONS = 0.05
EPSILON = 1e-06
AXES = ("head", "tail")
F32, BF16 = jnp.float32, jnp.bfloat16
ROWS, COLS = 0, 1
PACK_ROWS = 16
VMEM_LIMIT = 24 * 1024 * 1024
VMEM = pl.BlockSpec(memory_space=pltpu.VMEM)
SMEM = pl.BlockSpec(memory_space=pltpu.SMEM)


def dot(a, b, contract_a, contract_b):
    return lax.dot_general(
        a, b, (((contract_a,), (contract_b,)), ((), ())), preferred_element_type=F32
    )


def to_column(row):
    return jnp.broadcast_to(row, (128, row.shape[1])).T


def spread(column, width):
    return jnp.concatenate([column] * (width // column.shape[1]), axis=1)


def adagrad_rows(table, state_row, gradient):
    width = gradient.shape[1]
    mean = jnp.sum(gradient * gradient, axis=1, keepdims=True) * (1.0 / width)
    state = to_column(state_row) + mean
    factor = RATE_ROWS / (jnp.sqrt(state) + EPSILON)
    return table - gradient * spread(factor, width), state


def one_hot_rows(index_row, rows):
    n = index_row.shape[1]
    return (lax.broadcasted_iota(jnp.int32, (rows, n), 0) == index_row).astype(F32).astype(BF16)


def by_relation(x, rel_ref, k, blocks, relation):
    size = x.shape[0] // blocks
    parts = []
    for b in range(blocks):
        part = x[b * size : (b + 1) * size]
        parts.append(jnp.where(rel_ref[k, b] == relation, part, jnp.zeros_like(part)))
    return jnp.concatenate(parts, axis=0)


def restore_relations(nat_ref, lo_ref, hi_ref, rel_s):
    half = lo_ref.shape[0]
    own = 2 * half // nat_ref.shape[0]
    if own % PACK_ROWS:
        rel_s[:half] = lo_ref[...]
        rel_s[half:] = hi_ref[...]
        return
    for part, ref in enumerate((lo_ref, hi_ref)):
        for j in range(half // own):
            block = nat_ref[part * (half // own) + j]
            rel_s[pl.ds(pl.multiple_of(block * own, own), own)] = ref[j * own : (j + 1) * own]


def prepare_kernel(
    head_ref, tail_ref, hrows_ref, trows_ref, neg_ref, h_ref, t_ref, tcol_ref, cnt_ref
):
    buckets = hrows_ref.shape[0]
    blocks, nneg = neg_ref.shape[1:]
    pick = one_hot_rows(hrows_ref[0:1, :], head_ref.shape[0])
    h_ref[...] = dot(pick, head_ref[...].astype(BF16), ROWS, ROWS).astype(BF16)
    t_ref[...] = tail_ref[...].astype(BF16)
    ones = jnp.ones((8, nneg), BF16)
    for k in range(buckets):
        tcol_ref[k] = to_column(trows_ref[k : k + 1, :].astype(F32))
        for b in range(blocks):
            hot = one_hot_rows(neg_ref[k, b : b + 1, :], tail_ref.shape[0])
            cnt_ref[k, b : b + 1, :] = dot(ones, hot, COLS, COLS)[0:1, :]


def score_kernel(
    k, nneg, nat_ref, live_ref, rel_ref, lo_ref, hi_ref, h_ref, t_ref, tcol_ref, cnt_ref,
    keep_ref, send_ref, w_ref, u_ref, gu_ref, rel_s, grad_s,
):
    edges, width = h_ref.shape
    blocks, rows = cnt_ref.shape[1:]
    size = edges // blocks
    relations = rel_s.shape[0] // width
    restore_relations(nat_ref, lo_ref, hi_ref, rel_s)
    masked = [by_relation(h_ref[...], rel_ref, k, blocks, r) for r in range(relations)]
    u = dot(masked[0], rel_s[0:width], COLS, ROWS)
    for r in range(1, relations):
        u = u + dot(masked[r], rel_s[r * width : (r + 1) * width], COLS, ROWS)
    u = u.astype(BF16)
    u_ref[...] = u
    tails = t_ref[0:rows]
    score = dot(u, tails, COLS, COLS)
    row_id = lax.broadcasted_iota(jnp.int32, (size, rows), 1).astype(F32)
    for b in range(blocks):
        part = slice(b * size, (b + 1) * size)
        live = jnp.where(live_ref[k, 0] > b, 1.0, 0.0)
        half_tanh = 0.5 * jnp.tanh(0.5 * score[part])
        negative = ((0.5 + half_tanh) * (live / nneg)).astype(BF16).astype(F32)
        positive = (0.5 - half_tanh) * live
        is_tail = spread(tcol_ref[k, part], rows) == row_id
        weight = cnt_ref[k, b : b + 1, :] * negative - jnp.where(is_tail, positive, 0.0)
        w_ref[part] = weight.astype(BF16)
    gu = dot(w_ref[...], tails, COLS, ROWS).astype(BF16)
    gu_ref[...] = gu
    for r in range(relations):
        grad_s[r * width : (r + 1) * width] = dot(masked[r], gu, ROWS, ROWS)
    half = keep_ref.shape[0]
    own = 2 * half // nat_ref.shape[0]
    if own % PACK_ROWS:
        keep_ref[...] = grad_s[:half].astype(BF16)
        send_ref[...] = grad_s[half:].astype(BF16)
        return
    for part, ref in enumerate((keep_ref, send_ref)):
        for j in range(half // own):
            block = nat_ref[part * (half // own) + j]
            rows_of = pl.ds(pl.multiple_of(block * own, own), own)
            ref[j * own : (j + 1) * own] = grad_s[rows_of].astype(BF16)


def tail_kernel(w_ref, u_ref, table_ref, state_ref, out_ref):
    rows, width = table_ref.shape
    gradient = dot(w_ref[...], u_ref[...], ROWS, ROWS)
    table, state = adagrad_rows(table_ref[...], state_ref[...], gradient)
    out_ref[0:rows] = table.astype(BF16)
    state_row = state.T[0:1, :]
    high = state_row.astype(BF16).astype(F32)
    row_id = lax.broadcasted_iota(jnp.int32, (PACK_ROWS, width), 0)
    packed = jnp.where(row_id == 0, high, jnp.where(row_id == 1, state_row - high, 0.0))
    out_ref[rows : rows + PACK_ROWS] = packed.astype(BF16)


def last_tail_kernel(w_ref, u_ref, packed_ref, out_ref):
    rows = out_ref.shape[0]
    gradient = dot(w_ref[...], u_ref[...], ROWS, ROWS)
    packed = packed_ref[rows : rows + PACK_ROWS].astype(F32)
    state_row = packed[0:1, :] + packed[1:2, :]
    out_ref[...] = adagrad_rows(packed_ref[0:rows].astype(F32), state_row, gradient)[0]


def head_kernel(
    k, blocks, nat_ref, rel_ref, lo_ref, hi_ref, gu_ref, hrows_ref, table_ref, state_ref, *rest
):
    out_ref, rel_s = rest[0], rest[-1]
    rows, width = table_ref.shape
    relations = rel_s.shape[0] // width
    restore_relations(nat_ref, lo_ref, hi_ref, rel_s)
    gu = gu_ref[...]
    terms = None
    for r in range(relations):
        part = by_relation(gu, rel_ref, k, blocks, r)
        term = dot(part, rel_s[r * width : (r + 1) * width], COLS, COLS)
        terms = term if terms is None else terms + term
    hot = one_hot_rows(hrows_ref[k : k + 1, :], rows)
    gradient = dot(hot, terms.astype(BF16), COLS, ROWS)
    table, state = adagrad_rows(table_ref[...], state_ref[...], gradient)
    out_ref[...] = table
    if len(rest) > 2:
        state_out_ref, h_ref = rest[1:3]
        state_out_ref[...] = state.T[0:1, :]
        pick = one_hot_rows(hrows_ref[k + 1 : k + 2, :], rows)
        h_ref[...] = dot(pick, table.astype(BF16), ROWS, ROWS).astype(BF16)


def call(kernel, outs, smem, scratch, flops, *args):
    outs = [jax.ShapeDtypeStruct(shape, kind) for shape, kind in outs]
    moved = sum(a.size * a.dtype.itemsize for a in (*args, *outs))
    return pl.pallas_call(
        kernel,
        out_shape=outs,
        in_specs=[SMEM] * smem + [VMEM] * (len(args) - smem),
        out_specs=[VMEM] * len(outs),
        scratch_shapes=scratch,
        compiler_params=pltpu.CompilerParams(vmem_limit_bytes=VMEM_LIMIT),
        cost_estimate=pl.CostEstimate(flops=flops, bytes_accessed=moved, transcendentals=0),
    )(*args)


class Exchange:
    def __init__(self, heads, tails):
        self.devices = heads * tails
        head_bits = [tails << i for i in range(heads.bit_length() - 1)]
        tail_bits = [1 << i for i in range(tails.bit_length() - 1)]
        rest = head_bits[1:2] + tail_bits + head_bits[2:]
        self.stages = [head_bits[:1]] + [rest[i : i + 2] for i in range(0, len(rest), 2)]
        bits = [bit for stage in self.stages for bit in stage]
        places = [self.others(bits, j) for j in range(self.devices)]
        slots = np.zeros(self.devices, np.int32)
        slots[places] = np.arange(self.devices)
        me = lax.axis_index(AXES)
        self.block_of_slot = jnp.asarray(places, jnp.int32) ^ me
        self.slot_of_block = jnp.asarray(slots)[jnp.arange(self.devices, dtype=jnp.int32) ^ me]

    def others(self, bits, j):
        return sum(bit for i, bit in enumerate(bits) if j >> (len(bits) - 1 - i) & 1)

    def masks(self, stage):
        return [self.others(stage, j) for j in range(1, 1 << len(stage))]

    def swap(self, x, mask):
        return lax.ppermute(x, AXES, [(i, i ^ mask) for i in range(self.devices)])

    def reduce_scatter(self, keep, send, beside):
        if (2 * keep.shape[0] // self.devices) % PACK_ROWS:
            both = jnp.concatenate([keep, send])
            both = both.reshape(self.devices, -1, both.shape[1])[self.block_of_slot]
            keep, send = jnp.split(both.reshape(-1, both.shape[2]), 2)
        parts = [keep, send]
        for i, stage in enumerate(self.stages):
            got = [self.swap(part, mask) for part, mask in zip(parts[1:], self.masks(stage))]
            if i == 1:
                got, beside = lax.optimization_barrier((got, beside))
            pieces = parts[:1] + got
            if i + 1 == len(self.stages):
                return sum(piece.astype(F32) for piece in pieces), beside
            count = 1 << len(self.stages[i + 1])
            size = pieces[0].shape[0] // count
            parts = [
                sum(piece[j * size : (j + 1) * size].astype(F32) for piece in pieces).astype(BF16)
                for j in range(count)
            ]

    def all_gather(self, own, beside=()):
        rows = own.shape[0]
        for i, stage in reversed(list(enumerate(self.stages))[1:]):
            got = [self.swap(own, mask) for mask in self.masks(stage)]
            if i == 1:
                got, beside = lax.optimization_barrier((got, beside))
            own = jnp.concatenate([own] + got)
        lo, hi = own, self.swap(own, self.masks(self.stages[0])[0])
        if rows % PACK_ROWS:
            both = jnp.concatenate([lo, hi]).reshape(self.devices, rows, -1)[self.slot_of_block]
            lo, hi = jnp.split(both.reshape(self.devices * rows, -1), 2)
        return lo, hi, beside


def shards(
    head_table,
    head_state,
    tail_table,
    tail_state,
    relations,
    relation_state,
    head_rows,
    tail_rows,
    negatives,
    relation_ids,
    block_counts,
):
    heads, tails = lax.axis_size("head"), lax.axis_size("tail")
    exchange = Exchange(heads, tails)
    nat = exchange.block_of_slot
    rows, width = tail_table.shape
    edges = head_rows.shape[1]
    blocks, nneg = negatives.shape[1:]
    all_rows = relations.shape[0] * exchange.devices
    half = all_rows // 2
    square = 2 * rows * edges * width

    beside = call(
        prepare_kernel,
        [
            ((edges, width), BF16),
            ((rows, width), BF16),
            ((2, edges, 128), F32),
            ((2, blocks, rows), F32),
        ],
        0, [], square,
        head_table, tail_table, head_rows, tail_rows, negatives,
    )
    head_state = head_state.reshape(1, -1)
    tail_state = tail_state.reshape(1, -1)
    for k in range(2):
        lo, hi, beside = exchange.all_gather(relations.astype(BF16), beside)
        if k == 0:
            head_vecs, tail_vecs, tail_col, counts = beside
        keep, send, weights, projected, edge_grad = call(
            functools.partial(score_kernel, k, float(nneg)),
            [
                ((half, width), BF16),
                ((half, width), BF16),
                ((edges, rows), BF16),
                ((edges, width), BF16),
                ((edges, width), BF16),
            ],
            3, [pltpu.VMEM((all_rows, width), BF16), pltpu.VMEM((all_rows, width), F32)], 6 * square,
            nat, block_counts, relation_ids, lo, hi, head_vecs, tail_vecs, tail_col, counts,
        )
        head_outs = [(head_table.shape, F32)]
        if k == 0:
            tail_new = call(
                tail_kernel, [((rows + PACK_ROWS, width), BF16)], 0, [], square,
                weights, projected, tail_table, tail_state,
            )
            head_outs += [(head_state.shape, F32), ((edges, width), BF16)]
        else:
            tail_new = call(
                last_tail_kernel, [((rows, width), F32)], 0, [], square,
                weights, projected, tail_vecs,
            )
        head_new = call(
            functools.partial(head_kernel, k, blocks), head_outs,
            2, [pltpu.VMEM((all_rows, width), BF16)], 4 * square,
            nat, relation_ids, lo, hi, edge_grad, head_rows, head_table, head_state,
        )
        grad, ((tail_new,), head_new) = exchange.reduce_scatter(keep, send, (tail_new, head_new))
        if k == 0:
            head_table, head_state, head_vecs = head_new
            tail_vecs = lax.ppermute(tail_new, "tail", [(i, (i + 1) % tails) for i in range(tails)])
        relation_state = relation_state + grad * grad
        relations = relations - RATE_RELATIONS * grad / (jnp.sqrt(relation_state) + EPSILON)
        beside = ()
    return (head_new[0], tail_new, relations)


def solution(mesh):
    both = P(AXES, None)
    in_specs = (
        both,
        P(AXES),
        both,
        P(AXES),
        both,
        both,
        P(None, AXES),
        P(None, AXES),
        P(None, AXES, None),
        P(None, AXES),
        P(None, AXES),
    )
    return jax.shard_map(
        shards, mesh=mesh, in_specs=in_specs, out_specs=(both, both, both), check_vma=False
    )
```

```python
import functools

import jax
import jax.numpy as jnp
import numpy as np
from jax import lax
from jax.experimental import pallas as pl
from jax.experimental.pallas import tpu as pltpu
from jax.sharding import PartitionSpec as P

RATE_ROWS = 0.2
RATE_RELATIONS = 0.05
EPSILON = 1e-06
AXES = ("head", "tail")
F32, BF16 = jnp.float32, jnp.bfloat16
ROWS, COLS = 0, 1
PACK_ROWS = 16
VMEM_LIMIT = 24 * 1024 * 1024
VMEM = pl.BlockSpec(memory_space=pltpu.VMEM)
SMEM = pl.BlockSpec(memory_space=pltpu.SMEM)


def dot(a, b, contract_a, contract_b):
    return lax.dot_general(
        a, b, (((contract_a,), (contract_b,)), ((), ())), preferred_element_type=F32
    )


def to_column(row):
    return jnp.broadcast_to(row, (128, row.shape[1])).T


def spread(column, width):
    return jnp.concatenate([column] * (width // column.shape[1]), axis=1)


def adagrad_rows(table, state_row, gradient):
    width = gradient.shape[1]
    mean = jnp.sum(gradient * gradient, axis=1, keepdims=True) * (1.0 / width)
    state = to_column(state_row) + mean
    factor = RATE_ROWS / (jnp.sqrt(state) + EPSILON)
    return table - gradient * spread(factor, width), state


def one_hot_rows(index_row, rows):
    n = index_row.shape[1]
    return (lax.broadcasted_iota(jnp.int32, (rows, n), 0) == index_row).astype(F32).astype(BF16)


def by_relation(x, rel_ref, k, blocks, relation):
    size = x.shape[0] // blocks
    parts = []
    for b in range(blocks):
        part = x[b * size : (b + 1) * size]
        parts.append(jnp.where(rel_ref[k, b] == relation, part, jnp.zeros_like(part)))
    return jnp.concatenate(parts, axis=0)


def restore_relations(nat_ref, lo_ref, hi_ref, rel_s):
    half = lo_ref.shape[0]
    own = 2 * half // nat_ref.shape[0]
    if own % PACK_ROWS:
        rel_s[:half] = lo_ref[...]
        rel_s[half:] = hi_ref[...]
        return
    for part, ref in enumerate((lo_ref, hi_ref)):
        for j in range(half // own):
            block = nat_ref[part * (half // own) + j]
            rel_s[pl.ds(pl.multiple_of(block * own, own), own)] = ref[j * own : (j + 1) * own]


def prepare_kernel(
    head_ref, tail_ref, hrows_ref, trows_ref, neg_ref, h_ref, t_ref, tcol_ref, cnt_ref
):
    buckets = hrows_ref.shape[0]
    blocks, nneg = neg_ref.shape[1:]
    pick = one_hot_rows(hrows_ref[0:1, :], head_ref.shape[0])
    h_ref[...] = dot(pick, head_ref[...].astype(BF16), ROWS, ROWS).astype(BF16)
    t_ref[...] = tail_ref[...].astype(BF16)
    ones = jnp.ones((8, nneg), BF16)
    for k in range(buckets):
        tcol_ref[k] = to_column(trows_ref[k : k + 1, :].astype(F32))
        for b in range(blocks):
            hot = one_hot_rows(neg_ref[k, b : b + 1, :], tail_ref.shape[0])
            cnt_ref[k, b : b + 1, :] = dot(ones, hot, COLS, COLS)[0:1, :]


def score_kernel(
    k, nneg, nat_ref, live_ref, rel_ref, lo_ref, hi_ref, h_ref, tcol_ref, cnt_ref, *rest
):
    tail_refs, (keep_ref, send_ref, w_ref, u_ref, gu_ref, rel_s, grad_s) = rest[:-7], rest[-7:]
    edges, width = h_ref.shape
    blocks, rows = cnt_ref.shape[1:]
    size = edges // blocks
    relations = rel_s.shape[0] // width
    restore_relations(nat_ref, lo_ref, hi_ref, rel_s)
    masked = [by_relation(h_ref[...], rel_ref, k, blocks, r) for r in range(relations)]
    u = dot(masked[0], rel_s[0:width], COLS, ROWS)
    for r in range(1, relations):
        u = u + dot(masked[r], rel_s[r * width : (r + 1) * width], COLS, ROWS)
    u = u.astype(BF16)
    u_ref[...] = u
    tails = jnp.concatenate([ref[...] for ref in tail_refs])[0:rows]
    score = dot(u, tails, COLS, COLS)
    row_id = lax.broadcasted_iota(jnp.int32, (size, rows), 1).astype(F32)
    for b in range(blocks):
        part = slice(b * size, (b + 1) * size)
        live = jnp.where(live_ref[k, 0] > b, 1.0, 0.0)
        half_tanh = 0.5 * jnp.tanh(0.5 * score[part])
        negative = ((0.5 + half_tanh) * (live / nneg)).astype(BF16).astype(F32)
        positive = (0.5 - half_tanh) * live
        is_tail = spread(tcol_ref[k, part], rows) == row_id
        weight = cnt_ref[k, b : b + 1, :] * negative - jnp.where(is_tail, positive, 0.0)
        w_ref[part] = weight.astype(BF16)
    gu = dot(w_ref[...], tails, COLS, ROWS).astype(BF16)
    gu_ref[...] = gu
    for r in range(relations):
        grad_s[r * width : (r + 1) * width] = dot(masked[r], gu, ROWS, ROWS)
    half = keep_ref.shape[0]
    own = 2 * half // nat_ref.shape[0]
    if own % PACK_ROWS:
        keep_ref[...] = grad_s[:half].astype(BF16)
        send_ref[...] = grad_s[half:].astype(BF16)
        return
    for part, ref in enumerate((keep_ref, send_ref)):
        for j in range(half // own):
            block = nat_ref[part * (half // own) + j]
            rows_of = pl.ds(pl.multiple_of(block * own, own), own)
            ref[j * own : (j + 1) * own] = grad_s[rows_of].astype(BF16)


def tail_kernel(w_ref, u_ref, table_ref, state_ref, *out_refs):
    rows, width = table_ref.shape
    gradient = dot(w_ref[...], u_ref[...], ROWS, ROWS)
    table, state = adagrad_rows(table_ref[...], state_ref[...], gradient)
    state_row = state.T[0:1, :]
    high = state_row.astype(BF16).astype(F32)
    row_id = lax.broadcasted_iota(jnp.int32, (PACK_ROWS, width), 0)
    packed = jnp.where(row_id == 0, high, jnp.where(row_id == 1, state_row - high, 0.0))
    packed = jnp.concatenate([table, packed]).astype(BF16)
    start = 0
    for ref in out_refs:
        ref[...] = packed[start : start + ref.shape[0]]
        start += ref.shape[0]


def last_tail_kernel(w_ref, u_ref, *refs):
    tail_refs, out_ref = refs[:-1], refs[-1]
    rows = out_ref.shape[0]
    gradient = dot(w_ref[...], u_ref[...], ROWS, ROWS)
    packed = jnp.concatenate([ref[...] for ref in tail_refs]).astype(F32)
    state_row = packed[rows : rows + 1] + packed[rows + 1 : rows + 2]
    out_ref[...] = adagrad_rows(packed[0:rows], state_row, gradient)[0]


def head_kernel(
    k, blocks, nat_ref, rel_ref, lo_ref, hi_ref, gu_ref, hrows_ref, table_ref, state_ref, *rest
):
    out_ref, rel_s = rest[0], rest[-1]
    rows, width = table_ref.shape
    relations = rel_s.shape[0] // width
    restore_relations(nat_ref, lo_ref, hi_ref, rel_s)
    gu = gu_ref[...]
    terms = None
    for r in range(relations):
        part = by_relation(gu, rel_ref, k, blocks, r)
        term = dot(part, rel_s[r * width : (r + 1) * width], COLS, COLS)
        terms = term if terms is None else terms + term
    hot = one_hot_rows(hrows_ref[k : k + 1, :], rows)
    gradient = dot(hot, terms.astype(BF16), COLS, ROWS)
    table, state = adagrad_rows(table_ref[...], state_ref[...], gradient)
    out_ref[...] = table
    if len(rest) > 2:
        state_out_ref, h_ref = rest[1:3]
        state_out_ref[...] = state.T[0:1, :]
        pick = one_hot_rows(hrows_ref[k + 1 : k + 2, :], rows)
        h_ref[...] = dot(pick, table.astype(BF16), ROWS, ROWS).astype(BF16)


def call(kernel, outs, smem, scratch, flops, *args):
    outs = [jax.ShapeDtypeStruct(shape, kind) for shape, kind in outs]
    moved = sum(a.size * a.dtype.itemsize for a in (*args, *outs))
    return pl.pallas_call(
        kernel,
        out_shape=outs,
        in_specs=[SMEM] * smem + [VMEM] * (len(args) - smem),
        out_specs=[VMEM] * len(outs),
        scratch_shapes=scratch,
        compiler_params=pltpu.CompilerParams(vmem_limit_bytes=VMEM_LIMIT),
        cost_estimate=pl.CostEstimate(flops=flops, bytes_accessed=moved, transcendentals=0),
    )(*args)


class Exchange:
    def __init__(self, heads, tails):
        self.devices = heads * tails
        head_bits = [tails << i for i in range(heads.bit_length() - 1)]
        tail_bits = [1 << i for i in range(tails.bit_length() - 1)]
        rest = head_bits[1:2] + tail_bits + head_bits[2:]
        pairs = [rest[i : i + 2] for i in range(0, len(rest), 2)]
        self.stages = [head_bits[:1]] + pairs
        bits = head_bits[:1] + rest
        places = [self.others(bits, j) for j in range(self.devices)]
        slots = np.zeros(self.devices, np.int32)
        slots[places] = np.arange(self.devices)
        me = lax.axis_index(AXES)
        self.block_of_slot = jnp.asarray(places, jnp.int32) ^ me
        self.slot_of_block = jnp.asarray(slots)[jnp.arange(self.devices, dtype=jnp.int32) ^ me]

    def others(self, bits, j):
        return sum(bit for i, bit in enumerate(bits) if j >> (len(bits) - 1 - i) & 1)

    def masks(self, stage):
        return [self.others(stage, j) for j in range(1, 1 << len(stage))]

    def swap(self, x, mask):
        return lax.ppermute(x, AXES, [(i, i ^ mask) for i in range(self.devices)])

    def reduce_scatter(self, keep, send, hooks):
        if (2 * keep.shape[0] // self.devices) % PACK_ROWS:
            both = jnp.concatenate([keep, send])
            both = both.reshape(self.devices, -1, both.shape[1])[self.block_of_slot]
            keep, send = jnp.split(both.reshape(-1, both.shape[2]), 2)
        parts = [keep, send]
        for i, stage in enumerate(self.stages):
            got = [self.swap(part, mask) for part, mask in zip(parts[1:], self.masks(stage))]
            pieces = parts[:1] + hooks.get(i, list)(got)
            if i + 1 == len(self.stages):
                return sum(piece.astype(F32) for piece in pieces)
            count = 1 << len(self.stages[i + 1])
            size = pieces[0].shape[0] // count
            parts = [
                sum(piece[j * size : (j + 1) * size].astype(F32) for piece in pieces).astype(BF16)
                for j in range(count)
            ]

    def all_gather(self, own, hooks):
        rows = own.shape[0]
        for i, stage in reversed(list(enumerate(self.stages))[1:]):
            got = [self.swap(own, mask) for mask in self.masks(stage)]
            own = jnp.concatenate([own] + hooks.get(i, list)(got))
        lo, hi = own, self.swap(own, self.masks(self.stages[0])[0])
        if rows % PACK_ROWS:
            both = jnp.concatenate([lo, hi]).reshape(self.devices, rows, -1)[self.slot_of_block]
            lo, hi = jnp.split(both.reshape(self.devices * rows, -1), 2)
        return lo, hi


def shards(
    head_table,
    head_state,
    tail_table,
    tail_state,
    relations,
    relation_state,
    head_rows,
    tail_rows,
    negatives,
    relation_ids,
    block_counts,
):
    heads, tails = lax.axis_size("head"), lax.axis_size("tail")
    exchange = Exchange(heads, tails)
    nat = exchange.block_of_slot
    rows, width = tail_table.shape
    edges = head_rows.shape[1]
    blocks, nneg = negatives.shape[1:]
    all_rows = relations.shape[0] * exchange.devices
    half = all_rows // 2
    square = 2 * rows * edges * width

    prepared = call(
        prepare_kernel,
        [
            ((edges, width), BF16),
            ((rows, width), BF16),
            ((2, edges, 128), F32),
            ((2, blocks, rows), F32),
        ],
        0, [], square,
        head_table, tail_table, head_rows, tail_rows, negatives,
    )
    head_state = head_state.reshape(1, -1)
    tail_state = tail_state.reshape(1, -1)
    held = {"prepared": prepared}
    rotated = []

    def with_(name):
        def hook(got):
            got, held[name] = lax.optimization_barrier((got, held[name]))
            return got

        return hook

    def rotate(x, step):
        if step == 0:
            return lax.ppermute(x, "tail", [(i, (i + i % 2 * 2) % tails) for i in range(tails)])
        return lax.ppermute(x, "tail", [(i, i ^ 1) for i in range(tails)])

    def rotation(start, wait):
        def hook(got):
            if start is not None:
                got[0], part = lax.optimization_barrier((got[0], step0[start]))
                moved = rotate(part, 1)
            if wait is not None:
                got, rotated[wait] = lax.optimization_barrier((got, rotated[wait]))
            if start is not None:
                rotated.append(moved)
            return got

        return hook

    gather_hooks = {1: with_("prepared")}
    for k in range(2):
        lo, hi = exchange.all_gather(relations.astype(BF16), gather_hooks)
        if k == 0:
            head_vecs, *tail_vecs, tail_col, counts = held["prepared"]
        else:
            tail_vecs = rotated
        keep, send, weights, projected, edge_grad = call(
            functools.partial(score_kernel, k, float(nneg)),
            [
                ((half, width), BF16),
                ((half, width), BF16),
                ((edges, rows), BF16),
                ((edges, width), BF16),
                ((edges, width), BF16),
            ],
            3, [pltpu.VMEM((all_rows, width), BF16), pltpu.VMEM((all_rows, width), F32)], 6 * square,
            nat, block_counts, relation_ids, lo, hi, head_vecs, tail_col, counts, *tail_vecs,
        )
        head_outs = [(head_table.shape, F32)]
        if k == 0:
            tail_new = call(
                tail_kernel, [((n, width), BF16) for n in [rows + PACK_ROWS]], 0, [], square,
                weights, projected, tail_table, tail_state,
            )
            head_outs += [(head_state.shape, F32), ((edges, width), BF16)]
        else:
            tail_new = call(
                last_tail_kernel, [((rows, width), F32)], 0, [], square,
                weights, projected, *tail_vecs,
            )
        head_new = call(
            functools.partial(head_kernel, k, blocks), head_outs,
            2, [pltpu.VMEM((all_rows, width), BF16)], 4 * square,
            nat, relation_ids, lo, hi, edge_grad, head_rows, head_table, head_state,
        )
        held.update(tail=tail_new, head=list(head_new))
        if k == 0:
            step0 = []

            def begin(got):
                got = with_("tail")(got)
                step0.extend(rotate(x, 0) for x in held["tail"])
                return got

            hooks = {0: begin, 1: with_("head"), 2: rotation(0, None)}
        else:
            first, second = with_("tail"), with_("head")
            hooks = {1: lambda got: first(second(got))}
        grad = exchange.reduce_scatter(keep, send, hooks)
        if k == 0:
            head_table, head_state, head_vecs = held["head"]
            gather_hooks = {1: rotation(None, 0)}
        relation_state = relation_state + grad * grad
        relations = relations - RATE_RELATIONS * grad / (jnp.sqrt(relation_state) + EPSILON)
    return (held["head"][0], held["tail"][0], relations)


def solution(mesh):
    both = P(AXES, None)
    in_specs = (
        both,
        P(AXES),
        both,
        P(AXES),
        both,
        both,
        P(None, AXES),
        P(None, AXES),
        P(None, AXES, None),
        P(None, AXES),
        P(None, AXES),
    )
    return jax.shard_map(
        shards, mesh=mesh, in_specs=in_specs, out_specs=(both, both, both), check_vma=False
    )
```

```python
import functools

import jax
import jax.numpy as jnp
import numpy as np
from jax import lax
from jax.experimental import pallas as pl
from jax.experimental.pallas import tpu as pltpu
from jax.sharding import PartitionSpec as P

RATE_ROWS = 0.2
RATE_RELATIONS = 0.05
EPSILON = 1e-06
AXES = ("head", "tail")
F32, BF16 = jnp.float32, jnp.bfloat16
ROWS, COLS = 0, 1
PACK_ROWS = 16
VMEM_LIMIT = 24 * 1024 * 1024
VMEM = pl.BlockSpec(memory_space=pltpu.VMEM)
SMEM = pl.BlockSpec(memory_space=pltpu.SMEM)


def dot(a, b, contract_a, contract_b):
    return lax.dot_general(
        a, b, (((contract_a,), (contract_b,)), ((), ())), preferred_element_type=F32
    )


def to_column(row):
    return jnp.broadcast_to(row, (128, row.shape[1])).T


def spread(column, width):
    return jnp.concatenate([column] * (width // column.shape[1]), axis=1)


def adagrad_rows(table, state_row, gradient):
    width = gradient.shape[1]
    mean = jnp.sum(gradient * gradient, axis=1, keepdims=True) * (1.0 / width)
    state = to_column(state_row) + mean
    factor = RATE_ROWS / (jnp.sqrt(state) + EPSILON)
    return table - gradient * spread(factor, width), state


def one_hot_rows(index_row, rows):
    n = index_row.shape[1]
    return (lax.broadcasted_iota(jnp.int32, (rows, n), 0) == index_row).astype(F32).astype(BF16)


def restore_relations(nat_ref, lo_ref, hi_ref, rel_s, own):
    half = lo_ref.shape[0]
    if own % PACK_ROWS:
        rel_s[:half] = lo_ref[...]
        rel_s[half:] = hi_ref[...]
        return
    for part, ref in enumerate((lo_ref, hi_ref)):
        for j in range(half // own):
            block = nat_ref[part * (half // own) + j]
            rel_s[pl.ds(pl.multiple_of(block * own, own), own)] = ref[j * own : (j + 1) * own]


def prepare_kernel(
    head_ref, tail_ref, hrows_ref, trows_ref, neg_ref, h_ref, t_ref, tcol_ref, cnt_ref
):
    buckets = hrows_ref.shape[0]
    blocks, nneg = neg_ref.shape[1:]
    pick = one_hot_rows(hrows_ref[0:1, :], head_ref.shape[0])
    h_ref[...] = dot(pick, head_ref[...].astype(BF16), ROWS, ROWS).astype(BF16)
    t_ref[...] = tail_ref[...].astype(BF16)
    ones = jnp.ones((8, nneg), BF16)
    for k in range(buckets):
        tcol_ref[k] = to_column(trows_ref[k : k + 1, :].astype(F32))
        for b in range(blocks):
            hot = one_hot_rows(neg_ref[k, b : b + 1, :], tail_ref.shape[0])
            cnt_ref[k, b : b + 1, :] = dot(ones, hot, COLS, COLS)[0:1, :]


def score_kernel(
    k, own, nneg, nat_ref, live_ref, rel_ref, lo_ref, hi_ref, h_ref, tcol_ref, cnt_ref, *rest
):
    tail_refs, (keep_ref, send_ref, w_ref, u_ref, gu_ref, rel_s, grad_s) = rest[:-7], rest[-7:]
    edges, width = h_ref.shape
    blocks, rows = cnt_ref.shape[1:]
    size = edges // blocks
    relations = rel_s.shape[0] // width
    restore_relations(nat_ref, lo_ref, hi_ref, rel_s, own)
    half = keep_ref.shape[0]
    for b in range(blocks):
        part = slice(b * size, (b + 1) * size)
        chosen = rel_s[pl.ds(pl.multiple_of(rel_ref[k, b] * width, width), width)]
        u_ref[part] = dot(h_ref[part], chosen, COLS, ROWS).astype(BF16)
    tails = jnp.concatenate([ref[...] for ref in tail_refs])[0:rows]
    score = dot(u_ref[...], tails, COLS, COLS)
    row_id = lax.broadcasted_iota(jnp.int32, (size, rows), 1).astype(F32)
    for b in range(blocks):
        part = slice(b * size, (b + 1) * size)
        half_live = jnp.where(live_ref[k, 0] > b, 0.5, 0.0)
        share = cnt_ref[k, b : b + 1, :] * (half_live / nneg)
        t = jnp.tanh(0.5 * score[part])
        is_tail = spread(tcol_ref[k, part], rows) == row_id
        weight = (share + share * t) - jnp.where(is_tail, half_live - half_live * t, 0.0)
        w_ref[part] = weight.astype(BF16)
    gu = dot(w_ref[...], tails, COLS, ROWS).astype(BF16)
    gu_ref[...] = gu
    for r in range(relations):
        parts = []
        for b in range(blocks):
            part = h_ref[b * size : (b + 1) * size]
            parts.append(jnp.where(rel_ref[k, b] == r, part, jnp.zeros_like(part)))
        grad_s[r * width : (r + 1) * width] = dot(jnp.concatenate(parts), gu, ROWS, ROWS)
    if own % PACK_ROWS:
        keep_ref[...] = grad_s[:half].astype(BF16)
        send_ref[...] = grad_s[half:].astype(BF16)
        return
    for part, ref in enumerate((keep_ref, send_ref)):
        for j in range(half // own):
            block = nat_ref[part * (half // own) + j]
            rows_of = pl.ds(pl.multiple_of(block * own, own), own)
            ref[j * own : (j + 1) * own] = grad_s[rows_of].astype(BF16)


def tail_kernel(w_ref, u_ref, table_ref, state_ref, *out_refs):
    rows, width = table_ref.shape
    gradient = dot(w_ref[...], u_ref[...], ROWS, ROWS)
    table, state = adagrad_rows(table_ref[...], state_ref[...], gradient)
    state_row = state.T[0:1, :]
    high = state_row.astype(BF16).astype(F32)
    row_id = lax.broadcasted_iota(jnp.int32, (PACK_ROWS, width), 0)
    packed = jnp.where(row_id == 0, high, jnp.where(row_id == 1, state_row - high, 0.0))
    packed = jnp.concatenate([table, packed]).astype(BF16)
    start = 0
    for ref in out_refs:
        ref[...] = packed[start : start + ref.shape[0]]
        start += ref.shape[0]


def last_tail_kernel(w_ref, u_ref, *refs):
    tail_refs, out_ref = refs[:-1], refs[-1]
    rows = out_ref.shape[0]
    gradient = dot(w_ref[...], u_ref[...], ROWS, ROWS)
    packed = jnp.concatenate([ref[...] for ref in tail_refs]).astype(F32)
    state_row = packed[rows : rows + 1] + packed[rows + 1 : rows + 2]
    out_ref[...] = adagrad_rows(packed[0:rows], state_row, gradient)[0]


def head_kernel(
    k, own, blocks, nat_ref, rel_ref, lo_ref, hi_ref, gu_ref, hrows_ref, table_ref, state_ref, *rest
):
    out_ref, rel_s = rest[0], rest[-1]
    rows, width = table_ref.shape
    restore_relations(nat_ref, lo_ref, hi_ref, rel_s, own)
    size = gu_ref.shape[0] // blocks
    terms = []
    for b in range(blocks):
        chosen = rel_s[pl.ds(pl.multiple_of(rel_ref[k, b] * width, width), width)]
        terms.append(dot(gu_ref[b * size : (b + 1) * size], chosen, COLS, COLS).astype(BF16))
    hot = one_hot_rows(hrows_ref[k : k + 1, :], rows)
    gradient = dot(hot, jnp.concatenate(terms), COLS, ROWS)
    table, state = adagrad_rows(table_ref[...], state_ref[...], gradient)
    out_ref[...] = table
    if len(rest) > 2:
        state_out_ref, h_ref = rest[1:3]
        state_out_ref[...] = state.T[0:1, :]
        pick = one_hot_rows(hrows_ref[k + 1 : k + 2, :], rows)
        h_ref[...] = dot(pick, table.astype(BF16), ROWS, ROWS).astype(BF16)


def call(kernel, outs, smem, scratch, flops, *args):
    outs = [jax.ShapeDtypeStruct(shape, kind) for shape, kind in outs]
    moved = sum(a.size * a.dtype.itemsize for a in (*args, *outs))
    return pl.pallas_call(
        kernel,
        out_shape=outs,
        in_specs=[SMEM] * smem + [VMEM] * (len(args) - smem),
        out_specs=[VMEM] * len(outs),
        scratch_shapes=scratch,
        compiler_params=pltpu.CompilerParams(vmem_limit_bytes=VMEM_LIMIT),
        cost_estimate=pl.CostEstimate(flops=flops, bytes_accessed=moved, transcendentals=0),
    )(*args)


class Exchange:
    def __init__(self, heads, tails):
        self.devices = heads * tails
        head_bits = [tails << i for i in range(heads.bit_length() - 1)]
        tail_bits = [1 << i for i in range(tails.bit_length() - 1)]
        rest = head_bits[1:2] + tail_bits + head_bits[2:]
        pairs = [rest[i : i + 2] for i in range(0, len(rest), 2)]
        self.stages = [head_bits[:1]] + pairs
        bits = head_bits[:1] + rest
        places = [self.others(bits, j) for j in range(self.devices)]
        slots = np.zeros(self.devices, np.int32)
        slots[places] = np.arange(self.devices)
        me = lax.axis_index(AXES)
        self.block_of_slot = jnp.asarray(places, jnp.int32) ^ me
        self.slot_of_block = jnp.asarray(slots)[jnp.arange(self.devices, dtype=jnp.int32) ^ me]

    def others(self, bits, j):
        return sum(bit for i, bit in enumerate(bits) if j >> (len(bits) - 1 - i) & 1)

    def masks(self, stage):
        return [self.others(stage, j) for j in range(1, 1 << len(stage))]

    def swap(self, x, mask):
        return lax.ppermute(x, AXES, [(i, i ^ mask) for i in range(self.devices)])

    def reduce_scatter(self, keep, send, hooks):
        if (2 * keep.shape[0] // self.devices) % PACK_ROWS:
            both = jnp.concatenate([keep, send])
            both = both.reshape(self.devices, -1, both.shape[1])[self.block_of_slot]
            keep, send = jnp.split(both.reshape(-1, both.shape[2]), 2)
        parts = [keep, send]
        for i, stage in enumerate(self.stages):
            got = [self.swap(part, mask) for part, mask in zip(parts[1:], self.masks(stage))]
            pieces = parts[:1] + hooks.get(i, list)(got)
            if i + 1 == len(self.stages):
                return sum(piece.astype(F32) for piece in pieces)
            count = 1 << len(self.stages[i + 1])
            size = pieces[0].shape[0] // count
            parts = [
                sum(piece[j * size : (j + 1) * size].astype(F32) for piece in pieces).astype(BF16)
                for j in range(count)
            ]

    def all_gather(self, own, hooks):
        rows = own.shape[0]
        for i, stage in reversed(list(enumerate(self.stages))[1:]):
            got = [self.swap(own, mask) for mask in self.masks(stage)]
            own = jnp.concatenate([own] + hooks.get(i, list)(got))
        lo, hi = own, self.swap(own, self.masks(self.stages[0])[0])
        if rows % PACK_ROWS:
            both = jnp.concatenate([lo, hi]).reshape(self.devices, rows, -1)[self.slot_of_block]
            lo, hi = jnp.split(both.reshape(self.devices * rows, -1), 2)
        return lo, hi


def shards(
    head_table,
    head_state,
    tail_table,
    tail_state,
    relations,
    relation_state,
    head_rows,
    tail_rows,
    negatives,
    relation_ids,
    block_counts,
):
    heads, tails = lax.axis_size("head"), lax.axis_size("tail")
    exchange = Exchange(heads, tails)
    nat = exchange.block_of_slot
    own = relations.shape[0]
    rows, width = tail_table.shape
    edges = head_rows.shape[1]
    blocks, nneg = negatives.shape[1:]
    all_rows = relations.shape[0] * exchange.devices
    half = all_rows // 2
    square = 2 * rows * edges * width

    prepared = call(
        prepare_kernel,
        [
            ((edges, width), BF16),
            ((rows, width), BF16),
            ((2, edges, 128), F32),
            ((2, blocks, rows), F32),
        ],
        0, [], square,
        head_table, tail_table, head_rows, tail_rows, negatives,
    )
    head_state = head_state.reshape(1, -1)
    tail_state = tail_state.reshape(1, -1)
    held = {"prepared": prepared}
    rotated = []

    def with_(name):
        def hook(got):
            got, held[name] = lax.optimization_barrier((got, held[name]))
            return got

        return hook

    def rotate(x, step):
        if step == 0:
            return lax.ppermute(x, "tail", [(i, (i + i % 2 * 2) % tails) for i in range(tails)])
        return lax.ppermute(x, "tail", [(i, i ^ 1) for i in range(tails)])

    def rotation(start, wait):
        def hook(got):
            if start is not None:
                got[0], part = lax.optimization_barrier((got[0], step0[start]))
                moved = rotate(part, 1)
            if wait is not None:
                got, rotated[wait] = lax.optimization_barrier((got, rotated[wait]))
            if start is not None:
                rotated.append(moved)
            return got

        return hook

    gather_hooks = {1: with_("prepared")}
    for k in range(2):
        lo, hi = exchange.all_gather(relations.astype(BF16), gather_hooks)
        if k == 0:
            head_vecs, *tail_vecs, tail_col, counts = held["prepared"]
        else:
            tail_vecs = rotated
        keep, send, weights, projected, edge_grad = call(
            functools.partial(score_kernel, k, own, float(nneg)),
            [
                ((half, width), BF16),
                ((half, width), BF16),
                ((edges, rows), BF16),
                ((edges, width), BF16),
                ((edges, width), BF16),
            ],
            3, [pltpu.VMEM((all_rows, width), BF16), pltpu.VMEM((all_rows, width), F32)], 5 * square,
            nat, block_counts, relation_ids, lo, hi, head_vecs, tail_col, counts, *tail_vecs,
        )
        head_outs = [(head_table.shape, F32)]
        if k == 0:
            tail_new = call(
                tail_kernel, [((n, width), BF16) for n in [rows + PACK_ROWS]], 0, [], square,
                weights, projected, tail_table, tail_state,
            )
            head_outs += [(head_state.shape, F32), ((edges, width), BF16)]
        else:
            tail_new = call(
                last_tail_kernel, [((rows, width), F32)], 0, [], square,
                weights, projected, *tail_vecs,
            )
        head_new = call(
            functools.partial(head_kernel, k, own, blocks), head_outs,
            2, [pltpu.VMEM((all_rows, width), BF16)], 4 * square,
            nat, relation_ids, lo, hi, edge_grad, head_rows, head_table, head_state,
        )
        held.update(tail=tail_new, head=list(head_new))
        if k == 0:
            step0 = []

            def begin(got):
                got = with_("tail")(got)
                step0.extend(rotate(x, 0) for x in held["tail"])
                return got

            hooks = {0: begin, 1: with_("head"), 2: rotation(0, None)}
        else:
            first, second = with_("tail"), with_("head")
            hooks = {1: lambda got: first(second(got))}
        grad = exchange.reduce_scatter(keep, send, hooks)
        if k == 0:
            head_table, head_state, head_vecs = held["head"]
            gather_hooks = {1: rotation(None, 0)}
        relation_state = relation_state + grad * grad
        relations = relations - RATE_RELATIONS * grad / (jnp.sqrt(relation_state) + EPSILON)
    return (held["head"][0], held["tail"][0], relations)


def solution(mesh):
    both = P(AXES, None)
    in_specs = (
        both,
        P(AXES),
        both,
        P(AXES),
        both,
        both,
        P(None, AXES),
        P(None, AXES),
        P(None, AXES, None),
        P(None, AXES),
        P(None, AXES),
    )
    return jax.shard_map(
        shards, mesh=mesh, in_specs=in_specs, out_specs=(both, both, both), check_vma=False
    )
```

```python
import functools

import jax
import jax.numpy as jnp
import numpy as np
from jax import lax
from jax.experimental import pallas as pl
from jax.experimental.pallas import tpu as pltpu
from jax.sharding import PartitionSpec as P

RATE_ROWS = 0.2
RATE_RELATIONS = 0.05
EPSILON = 1e-06
AXES = ("head", "tail")
F32, BF16 = jnp.float32, jnp.bfloat16
ROWS, COLS = 0, 1
PACK_ROWS = 16
VMEM_LIMIT = 24 * 1024 * 1024
VMEM = pl.BlockSpec(memory_space=pltpu.VMEM)
SMEM = pl.BlockSpec(memory_space=pltpu.SMEM)


def dot(a, b, contract_a, contract_b):
    return lax.dot_general(
        a, b, (((contract_a,), (contract_b,)), ((), ())), preferred_element_type=F32
    )


def to_column(row):
    return jnp.broadcast_to(row, (128, row.shape[1])).T


def spread(column, width):
    return jnp.concatenate([column] * (width // column.shape[1]), axis=1)


def adagrad_rows(table, state_row, gradient):
    width = gradient.shape[1]
    mean = jnp.sum(gradient * gradient, axis=1, keepdims=True) * (1.0 / width)
    state = to_column(state_row) + mean
    factor = RATE_ROWS / (jnp.sqrt(state) + EPSILON)
    return table - gradient * spread(factor, width), state


def one_hot_rows(index_row, rows):
    n = index_row.shape[1]
    return (lax.broadcasted_iota(jnp.int32, (rows, n), 0) == index_row).astype(F32).astype(BF16)


def restore_relations(nat_ref, lo_ref, hi_ref, rel_s, own):
    half = lo_ref.shape[0]
    if own % PACK_ROWS:
        rel_s[:half] = lo_ref[...]
        rel_s[half:] = hi_ref[...]
        return
    for part, ref in enumerate((lo_ref, hi_ref)):
        for j in range(half // own):
            block = nat_ref[part * (half // own) + j]
            rel_s[pl.ds(pl.multiple_of(block * own, own), own)] = ref[j * own : (j + 1) * own]


def prepare_kernel(
    head_ref, tail_ref, hrows_ref, trows_ref, neg_ref, hstate_ref, tstate_ref,
    h_ref, t_ref, tcol_ref, cnt_ref, hstate_out_ref, tstate_out_ref,
):
    hstate_out_ref[...] = hstate_ref[...]
    tstate_out_ref[...] = tstate_ref[...]
    buckets = hrows_ref.shape[0]
    blocks, nneg = neg_ref.shape[1:]
    pick = one_hot_rows(hrows_ref[0:1, :], head_ref.shape[0])
    h_ref[...] = dot(pick, head_ref[...].astype(BF16), ROWS, ROWS).astype(BF16)
    t_ref[...] = tail_ref[...].astype(BF16)
    ones = jnp.ones((8, nneg), BF16)
    for k in range(buckets):
        tcol_ref[k] = to_column(trows_ref[k : k + 1, :].astype(F32))
        for b in range(blocks):
            hot = one_hot_rows(neg_ref[k, b : b + 1, :], tail_ref.shape[0])
            cnt_ref[k, b : b + 1, :] = dot(ones, hot, COLS, COLS)[0:1, :]


def score_kernel(
    k, own, nneg, nat_ref, live_ref, rel_ref, lo_ref, hi_ref, h_ref, tcol_ref, cnt_ref, *rest
):
    tail_refs, (keep_ref, send_ref, w_ref, u_ref, gu_ref, rel_s, grad_s) = rest[:-7], rest[-7:]
    edges, width = h_ref.shape
    blocks, rows = cnt_ref.shape[1:]
    size = edges // blocks
    relations = rel_s.shape[0] // width
    restore_relations(nat_ref, lo_ref, hi_ref, rel_s, own)
    half = keep_ref.shape[0]
    for b in range(blocks):
        part = slice(b * size, (b + 1) * size)
        chosen = rel_s[pl.ds(pl.multiple_of(rel_ref[k, b] * width, width), width)]
        u_ref[part] = dot(h_ref[part], chosen, COLS, ROWS).astype(BF16)
    tails = jnp.concatenate([ref[...] for ref in tail_refs])[0:rows]
    score = dot(u_ref[...], tails, COLS, COLS)
    row_id = lax.broadcasted_iota(jnp.int32, (size, rows), 1).astype(F32)
    for b in range(blocks):
        part = slice(b * size, (b + 1) * size)
        half_live = jnp.where(live_ref[k, 0] > b, 0.5, 0.0)
        share = cnt_ref[k, b : b + 1, :] * (half_live / nneg)
        t = jnp.tanh(0.5 * score[part])
        is_tail = spread(tcol_ref[k, part], rows) == row_id
        weight = (share + share * t) - jnp.where(is_tail, half_live - half_live * t, 0.0)
        w_ref[part] = weight.astype(BF16)
    gu = dot(w_ref[...], tails, COLS, ROWS).astype(BF16)
    gu_ref[...] = gu
    for r in range(relations):
        parts = []
        for b in range(blocks):
            part = h_ref[b * size : (b + 1) * size]
            parts.append(jnp.where(rel_ref[k, b] == r, part, jnp.zeros_like(part)))
        grad_s[r * width : (r + 1) * width] = dot(jnp.concatenate(parts), gu, ROWS, ROWS)
    if own % PACK_ROWS:
        keep_ref[...] = grad_s[:half].astype(BF16)
        send_ref[...] = grad_s[half:].astype(BF16)
        return
    for part, ref in enumerate((keep_ref, send_ref)):
        for j in range(half // own):
            block = nat_ref[part * (half // own) + j]
            rows_of = pl.ds(pl.multiple_of(block * own, own), own)
            ref[j * own : (j + 1) * own] = grad_s[rows_of].astype(BF16)


def tail_kernel(w_ref, u_ref, table_ref, state_ref, *out_refs):
    rows, width = table_ref.shape
    gradient = dot(w_ref[...], u_ref[...], ROWS, ROWS)
    table, state = adagrad_rows(table_ref[...], state_ref[...], gradient)
    state_row = state.T[0:1, :]
    high = state_row.astype(BF16).astype(F32)
    row_id = lax.broadcasted_iota(jnp.int32, (PACK_ROWS, width), 0)
    packed = jnp.where(row_id == 0, high, jnp.where(row_id == 1, state_row - high, 0.0))
    packed = jnp.concatenate([table, packed]).astype(BF16)
    start = 0
    for ref in out_refs:
        ref[...] = packed[start : start + ref.shape[0]]
        start += ref.shape[0]


def last_tail_kernel(w_ref, u_ref, *refs):
    tail_refs, out_ref = refs[:-1], refs[-1]
    rows = out_ref.shape[0]
    gradient = dot(w_ref[...], u_ref[...], ROWS, ROWS)
    packed = jnp.concatenate([ref[...] for ref in tail_refs]).astype(F32)
    state_row = packed[rows : rows + 1] + packed[rows + 1 : rows + 2]
    out_ref[...] = adagrad_rows(packed[0:rows], state_row, gradient)[0]


def head_kernel(
    k, own, blocks, nat_ref, rel_ref, lo_ref, hi_ref, gu_ref, hrows_ref, table_ref, state_ref, *rest
):
    out_ref, rel_s = rest[0], rest[-1]
    rows, width = table_ref.shape
    restore_relations(nat_ref, lo_ref, hi_ref, rel_s, own)
    size = gu_ref.shape[0] // blocks
    terms = []
    for b in range(blocks):
        chosen = rel_s[pl.ds(pl.multiple_of(rel_ref[k, b] * width, width), width)]
        terms.append(dot(gu_ref[b * size : (b + 1) * size], chosen, COLS, COLS).astype(BF16))
    hot = one_hot_rows(hrows_ref[k : k + 1, :], rows)
    gradient = dot(hot, jnp.concatenate(terms), COLS, ROWS)
    table, state = adagrad_rows(table_ref[...], state_ref[...], gradient)
    out_ref[...] = table
    if len(rest) > 2:
        state_out_ref, h_ref = rest[1:3]
        state_out_ref[...] = state.T[0:1, :]
        pick = one_hot_rows(hrows_ref[k + 1 : k + 2, :], rows)
        h_ref[...] = dot(pick, table.astype(BF16), ROWS, ROWS).astype(BF16)


def call(kernel, outs, smem, scratch, flops, *args):
    outs = [jax.ShapeDtypeStruct(shape, kind) for shape, kind in outs]
    moved = sum(a.size * a.dtype.itemsize for a in (*args, *outs))
    return pl.pallas_call(
        kernel,
        out_shape=outs,
        in_specs=[SMEM] * smem + [VMEM] * (len(args) - smem),
        out_specs=[VMEM] * len(outs),
        scratch_shapes=scratch,
        compiler_params=pltpu.CompilerParams(vmem_limit_bytes=VMEM_LIMIT),
        cost_estimate=pl.CostEstimate(flops=flops, bytes_accessed=moved, transcendentals=0),
    )(*args)


class Exchange:
    def __init__(self, heads, tails):
        self.devices = heads * tails
        head_bits = [tails << i for i in range(heads.bit_length() - 1)]
        tail_bits = [1 << i for i in range(tails.bit_length() - 1)]
        rest = head_bits[1:2] + tail_bits + head_bits[2:]
        pairs = [rest[i : i + 2] for i in range(0, len(rest), 2)]
        self.stages = [head_bits[:1]] + pairs
        bits = head_bits[:1] + rest
        places = [self.others(bits, j) for j in range(self.devices)]
        slots = np.zeros(self.devices, np.int32)
        slots[places] = np.arange(self.devices)
        me = lax.axis_index(AXES)
        self.block_of_slot = jnp.asarray(places, jnp.int32) ^ me
        self.slot_of_block = jnp.asarray(slots)[jnp.arange(self.devices, dtype=jnp.int32) ^ me]

    def others(self, bits, j):
        return sum(bit for i, bit in enumerate(bits) if j >> (len(bits) - 1 - i) & 1)

    def masks(self, stage):
        return [self.others(stage, j) for j in range(1, 1 << len(stage))]

    def swap(self, x, mask):
        return lax.ppermute(x, AXES, [(i, i ^ mask) for i in range(self.devices)])

    def reduce_scatter(self, keep, send, hooks):
        if (2 * keep.shape[0] // self.devices) % PACK_ROWS:
            both = jnp.concatenate([keep, send])
            both = both.reshape(self.devices, -1, both.shape[1])[self.block_of_slot]
            keep, send = jnp.split(both.reshape(-1, both.shape[2]), 2)
        parts = [keep, send]
        for i, stage in enumerate(self.stages):
            got = [self.swap(part, mask) for part, mask in zip(parts[1:], self.masks(stage))]
            pieces = parts[:1] + hooks.get(i, list)(got)
            if i + 1 == len(self.stages):
                return sum(piece.astype(F32) for piece in pieces)
            count = 1 << len(self.stages[i + 1])
            size = pieces[0].shape[0] // count
            parts = [
                sum(piece[j * size : (j + 1) * size].astype(F32) for piece in pieces).astype(BF16)
                for j in range(count)
            ]

    def all_gather(self, own, hooks):
        rows = own.shape[0]
        for i, stage in reversed(list(enumerate(self.stages))[1:]):
            got = [self.swap(own, mask) for mask in self.masks(stage)]
            own = jnp.concatenate([own] + hooks.get(i, list)(got))
        lo, hi = own, self.swap(own, self.masks(self.stages[0])[0])
        if rows % PACK_ROWS:
            both = jnp.concatenate([lo, hi]).reshape(self.devices, rows, -1)[self.slot_of_block]
            lo, hi = jnp.split(both.reshape(self.devices * rows, -1), 2)
        return lo, hi


def shards(
    head_table,
    head_state,
    tail_table,
    tail_state,
    relations,
    relation_state,
    head_rows,
    tail_rows,
    negatives,
    relation_ids,
    block_counts,
):
    heads, tails = lax.axis_size("head"), lax.axis_size("tail")
    exchange = Exchange(heads, tails)
    nat = exchange.block_of_slot
    own = relations.shape[0]
    rows, width = tail_table.shape
    edges = head_rows.shape[1]
    blocks, nneg = negatives.shape[1:]
    all_rows = relations.shape[0] * exchange.devices
    half = all_rows // 2
    square = 2 * rows * edges * width

    head_state = head_state.reshape(1, -1)
    tail_state = tail_state.reshape(1, -1)
    prepared = call(
        prepare_kernel,
        [
            ((edges, width), BF16),
            ((rows, width), BF16),
            ((2, edges, 128), F32),
            ((2, blocks, rows), F32),
            (head_state.shape, F32),
            (tail_state.shape, F32),
        ],
        0, [], square,
        head_table, tail_table, head_rows, tail_rows, negatives, head_state, tail_state,
    )
    held = {"prepared": prepared}
    rotated = []

    def with_(name):
        def hook(got):
            got, held[name] = lax.optimization_barrier((got, held[name]))
            return got

        return hook

    def rotate(x, step):
        if step == 0:
            return lax.ppermute(x, "tail", [(i, (i + i % 2 * 2) % tails) for i in range(tails)])
        return lax.ppermute(x, "tail", [(i, i ^ 1) for i in range(tails)])

    def rotation(start, wait):
        def hook(got):
            if start is not None:
                got[0], part = lax.optimization_barrier((got[0], step0[start]))
                moved = rotate(part, 1)
            if wait is not None:
                got, rotated[wait] = lax.optimization_barrier((got, rotated[wait]))
            if start is not None:
                rotated.append(moved)
            return got

        return hook

    gather_hooks = {1: with_("prepared")}
    for k in range(2):
        lo, hi = exchange.all_gather(relations.astype(BF16), gather_hooks)
        if k == 0:
            head_vecs, *tail_vecs, tail_col, counts, head_state, tail_state = held["prepared"]
        else:
            tail_vecs = rotated
        keep, send, weights, projected, edge_grad = call(
            functools.partial(score_kernel, k, own, float(nneg)),
            [
                ((half, width), BF16),
                ((half, width), BF16),
                ((edges, rows), BF16),
                ((edges, width), BF16),
                ((edges, width), BF16),
            ],
            3, [pltpu.VMEM((all_rows, width), BF16), pltpu.VMEM((all_rows, width), F32)], 5 * square,
            nat, block_counts, relation_ids, lo, hi, head_vecs, tail_col, counts, *tail_vecs,
        )
        head_outs = [(head_table.shape, F32)]
        if k == 0:
            tail_new = call(
                tail_kernel, [((n, width), BF16) for n in [rows + PACK_ROWS]], 0, [], square,
                weights, projected, tail_table, tail_state,
            )
            head_outs += [(head_state.shape, F32), ((edges, width), BF16)]
        else:
            tail_new = call(
                last_tail_kernel, [((rows, width), F32)], 0, [], square,
                weights, projected, *tail_vecs,
            )
        head_new = call(
            functools.partial(head_kernel, k, own, blocks), head_outs,
            2, [pltpu.VMEM((all_rows, width), BF16)], 4 * square,
            nat, relation_ids, lo, hi, edge_grad, head_rows, head_table, head_state,
        )
        held.update(tail=tail_new, head=list(head_new))
        if k == 0:
            step0 = [rotate(x, 0) for x in tail_new]
            hooks = {1: with_("head"), 2: rotation(0, None)}
        else:
            first, second = with_("tail"), with_("head")
            hooks = {1: lambda got: first(second(got))}
        grad = exchange.reduce_scatter(keep, send, hooks)
        if k == 0:
            head_table, head_state, head_vecs = held["head"]
            gather_hooks = {1: rotation(None, 0)}
        relation_state = relation_state + grad * grad
        relations = relations - RATE_RELATIONS * grad / (jnp.sqrt(relation_state) + EPSILON)
    return (held["head"][0], held["tail"][0], relations)


def solution(mesh):
    both = P(AXES, None)
    in_specs = (
        both,
        P(AXES),
        both,
        P(AXES),
        both,
        both,
        P(None, AXES),
        P(None, AXES),
        P(None, AXES, None),
        P(None, AXES),
        P(None, AXES),
    )
    return jax.shard_map(
        shards, mesh=mesh, in_specs=in_specs, out_specs=(both, both, both), check_vma=False
    )
```

```python
import functools

import jax
import jax.numpy as jnp
import numpy as np
from jax import lax
from jax.experimental import pallas as pl
from jax.experimental.pallas import tpu as pltpu
from jax.sharding import PartitionSpec as P

RATE_ROWS = 0.2
RATE_RELATIONS = 0.05
EPSILON = 1e-06
AXES = ("head", "tail")
F32, BF16 = jnp.float32, jnp.bfloat16
ROWS, COLS = 0, 1
PACK_ROWS = 16
VMEM_LIMIT = 24 * 1024 * 1024
VMEM = pl.BlockSpec(memory_space=pltpu.VMEM)
SMEM = pl.BlockSpec(memory_space=pltpu.SMEM)


def dot(a, b, contract_a, contract_b):
    return lax.dot_general(
        a, b, (((contract_a,), (contract_b,)), ((), ())), preferred_element_type=F32
    )


def to_column(row):
    return jnp.broadcast_to(row, (128, row.shape[1])).T


def spread(column, width):
    return jnp.concatenate([column] * (width // column.shape[1]), axis=1)


def adagrad_rows(table, state_row, gradient):
    width = gradient.shape[1]
    mean = jnp.sum(gradient * gradient, axis=1, keepdims=True) * (1.0 / width)
    state = to_column(state_row) + mean
    factor = RATE_ROWS / (jnp.sqrt(state) + EPSILON)
    return table - gradient * spread(factor, width), state


def one_hot_rows(index_row, rows):
    n = index_row.shape[1]
    return (lax.broadcasted_iota(jnp.int32, (rows, n), 0) == index_row).astype(F32).astype(BF16)


def restore_relations(nat_ref, lo_ref, hi_ref, rel_s, own):
    half = lo_ref.shape[0]
    if own % PACK_ROWS:
        rel_s[:half] = lo_ref[...]
        rel_s[half:] = hi_ref[...]
        return
    for part, ref in enumerate((lo_ref, hi_ref)):
        for j in range(half // own):
            block = nat_ref[part * (half // own) + j]
            rel_s[pl.ds(pl.multiple_of(block * own, own), own)] = ref[j * own : (j + 1) * own]


def prepare_kernel(
    head_ref, tail_ref, hrows_ref, trows_ref, neg_ref, hstate_ref, tstate_ref,
    h_ref, t_ref, tcol_ref, cnt_ref, hstate_out_ref, tstate_out_ref,
):
    hstate_out_ref[...] = hstate_ref[...]
    tstate_out_ref[...] = tstate_ref[...]
    buckets = hrows_ref.shape[0]
    blocks, nneg = neg_ref.shape[1:]
    pick = one_hot_rows(hrows_ref[0:1, :], head_ref.shape[0])
    h_ref[...] = dot(pick, head_ref[...].astype(BF16), ROWS, ROWS).astype(BF16)
    t_ref[...] = tail_ref[...].astype(BF16)
    ones = jnp.ones((8, nneg), BF16)
    for k in range(buckets):
        tcol_ref[k] = to_column(trows_ref[k : k + 1, :].astype(F32))
        for b in range(blocks):
            hot = one_hot_rows(neg_ref[k, b : b + 1, :], tail_ref.shape[0])
            cnt_ref[k, b : b + 1, :] = dot(ones, hot, COLS, COLS)[0:1, :]


def score_kernel(
    k, own, nneg, nat_ref, live_ref, rel_ref, lo_ref, hi_ref, h_ref, t_ref, tcol_ref, cnt_ref,
    keep_ref, send_ref, w_ref, u_ref, gu_ref, rel_s, grad_s,
):
    edges, width = h_ref.shape
    blocks, rows = cnt_ref.shape[1:]
    size = edges // blocks
    relations = rel_s.shape[0] // width
    restore_relations(nat_ref, lo_ref, hi_ref, rel_s, own)
    half = keep_ref.shape[0]
    for b in range(blocks):
        part = slice(b * size, (b + 1) * size)
        chosen = rel_s[pl.ds(pl.multiple_of(rel_ref[k, b] * width, width), width)]
        u_ref[part] = dot(h_ref[part], chosen, COLS, ROWS).astype(BF16)
    tails = t_ref[0:rows]
    score = dot(u_ref[...], tails, COLS, COLS)
    row_id = lax.broadcasted_iota(jnp.int32, (size, rows), 1).astype(F32)
    for b in range(blocks):
        part = slice(b * size, (b + 1) * size)
        half_live = jnp.where(live_ref[k, 0] > b, 0.5, 0.0)
        share = cnt_ref[k, b : b + 1, :] * (half_live / nneg)
        t = jnp.tanh(0.5 * score[part])
        is_tail = spread(tcol_ref[k, part], rows) == row_id
        weight = (share + share * t) - jnp.where(is_tail, half_live - half_live * t, 0.0)
        w_ref[part] = weight.astype(BF16)
    gu = dot(w_ref[...], tails, COLS, ROWS).astype(BF16)
    gu_ref[...] = gu
    for r in range(relations):
        parts = []
        for b in range(blocks):
            part = h_ref[b * size : (b + 1) * size]
            parts.append(jnp.where(rel_ref[k, b] == r, part, jnp.zeros_like(part)))
        grad_s[r * width : (r + 1) * width] = dot(jnp.concatenate(parts), gu, ROWS, ROWS)
    if own % PACK_ROWS:
        keep_ref[...] = grad_s[:half].astype(BF16)
        send_ref[...] = grad_s[half:].astype(BF16)
        return
    for part, ref in enumerate((keep_ref, send_ref)):
        for j in range(half // own):
            block = nat_ref[part * (half // own) + j]
            rows_of = pl.ds(pl.multiple_of(block * own, own), own)
            ref[j * own : (j + 1) * own] = grad_s[rows_of].astype(BF16)


def tail_kernel(w_ref, u_ref, table_ref, state_ref, out_ref):
    rows, width = table_ref.shape
    gradient = dot(w_ref[...], u_ref[...], ROWS, ROWS)
    table, state = adagrad_rows(table_ref[...], state_ref[...], gradient)
    out_ref[0:rows] = table.astype(BF16)
    state_row = state.T[0:1, :]
    high = state_row.astype(BF16).astype(F32)
    row_id = lax.broadcasted_iota(jnp.int32, (PACK_ROWS, width), 0)
    packed = jnp.where(row_id == 0, high, jnp.where(row_id == 1, state_row - high, 0.0))
    out_ref[rows : rows + PACK_ROWS] = packed.astype(BF16)


def last_tail_kernel(w_ref, u_ref, packed_ref, out_ref):
    rows = out_ref.shape[0]
    gradient = dot(w_ref[...], u_ref[...], ROWS, ROWS)
    packed = packed_ref[rows : rows + PACK_ROWS].astype(F32)
    state_row = packed[0:1, :] + packed[1:2, :]
    out_ref[...] = adagrad_rows(packed_ref[0:rows].astype(F32), state_row, gradient)[0]


def head_kernel(
    k, own, blocks, nat_ref, rel_ref, lo_ref, hi_ref, gu_ref, hrows_ref, table_ref, state_ref, *rest
):
    out_ref, rel_s = rest[0], rest[-1]
    rows, width = table_ref.shape
    restore_relations(nat_ref, lo_ref, hi_ref, rel_s, own)
    size = gu_ref.shape[0] // blocks
    terms = []
    for b in range(blocks):
        chosen = rel_s[pl.ds(pl.multiple_of(rel_ref[k, b] * width, width), width)]
        terms.append(dot(gu_ref[b * size : (b + 1) * size], chosen, COLS, COLS).astype(BF16))
    hot = one_hot_rows(hrows_ref[k : k + 1, :], rows)
    gradient = dot(hot, jnp.concatenate(terms), COLS, ROWS)
    table, state = adagrad_rows(table_ref[...], state_ref[...], gradient)
    out_ref[...] = table
    if len(rest) > 2:
        state_out_ref, h_ref = rest[1:3]
        state_out_ref[...] = state.T[0:1, :]
        pick = one_hot_rows(hrows_ref[k + 1 : k + 2, :], rows)
        h_ref[...] = dot(pick, table.astype(BF16), ROWS, ROWS).astype(BF16)


def call(kernel, outs, smem, scratch, flops, *args):
    outs = [jax.ShapeDtypeStruct(shape, kind) for shape, kind in outs]
    moved = sum(a.size * a.dtype.itemsize for a in (*args, *outs))
    return pl.pallas_call(
        kernel,
        out_shape=outs,
        in_specs=[SMEM] * smem + [VMEM] * (len(args) - smem),
        out_specs=[VMEM] * len(outs),
        scratch_shapes=scratch,
        compiler_params=pltpu.CompilerParams(vmem_limit_bytes=VMEM_LIMIT),
        cost_estimate=pl.CostEstimate(flops=flops, bytes_accessed=moved, transcendentals=0),
    )(*args)


class Exchange:
    def __init__(self, heads, tails):
        self.devices = heads * tails
        head_bits = [tails << i for i in range(heads.bit_length() - 1)]
        tail_bits = [1 << i for i in range(tails.bit_length() - 1)]
        rest = head_bits[1:2] + tail_bits + head_bits[2:]
        pairs = [rest[i : i + 2] for i in range(0, len(rest), 2)]
        self.stages = [head_bits[:1]] + pairs
        bits = head_bits[:1] + rest
        places = [self.others(bits, j) for j in range(self.devices)]
        slots = np.zeros(self.devices, np.int32)
        slots[places] = np.arange(self.devices)
        me = lax.axis_index(AXES)
        self.block_of_slot = jnp.asarray(places, jnp.int32) ^ me
        self.slot_of_block = jnp.asarray(slots)[jnp.arange(self.devices, dtype=jnp.int32) ^ me]

    def others(self, bits, j):
        return sum(bit for i, bit in enumerate(bits) if j >> (len(bits) - 1 - i) & 1)

    def masks(self, stage):
        return [self.others(stage, j) for j in range(1, 1 << len(stage))]

    def swap(self, x, mask):
        return lax.ppermute(x, AXES, [(i, i ^ mask) for i in range(self.devices)])

    def reduce_scatter(self, keep, send, hooks):
        if (2 * keep.shape[0] // self.devices) % PACK_ROWS:
            both = jnp.concatenate([keep, send])
            both = both.reshape(self.devices, -1, both.shape[1])[self.block_of_slot]
            keep, send = jnp.split(both.reshape(-1, both.shape[2]), 2)
        parts = [keep, send]
        for i, stage in enumerate(self.stages):
            got = [self.swap(part, mask) for part, mask in zip(parts[1:], self.masks(stage))]
            pieces = parts[:1] + hooks.get(i, list)(got)
            if i + 1 == len(self.stages):
                return sum(piece.astype(F32) for piece in pieces)
            count = 1 << len(self.stages[i + 1])
            size = pieces[0].shape[0] // count
            parts = [
                sum(piece[j * size : (j + 1) * size].astype(F32) for piece in pieces).astype(BF16)
                for j in range(count)
            ]

    def all_gather(self, own, hooks):
        rows = own.shape[0]
        for i, stage in reversed(list(enumerate(self.stages))[1:]):
            got = [self.swap(own, mask) for mask in self.masks(stage)]
            own = jnp.concatenate([own] + hooks.get(i, list)(got))
        lo, hi = own, self.swap(own, self.masks(self.stages[0])[0])
        if rows % PACK_ROWS:
            both = jnp.concatenate([lo, hi]).reshape(self.devices, rows, -1)[self.slot_of_block]
            lo, hi = jnp.split(both.reshape(self.devices * rows, -1), 2)
        return lo, hi


def shards(
    head_table,
    head_state,
    tail_table,
    tail_state,
    relations,
    relation_state,
    head_rows,
    tail_rows,
    negatives,
    relation_ids,
    block_counts,
):
    heads, tails = lax.axis_size("head"), lax.axis_size("tail")
    exchange = Exchange(heads, tails)
    nat = exchange.block_of_slot
    own = relations.shape[0]
    rows, width = tail_table.shape
    edges = head_rows.shape[1]
    blocks, nneg = negatives.shape[1:]
    all_rows = relations.shape[0] * exchange.devices
    half = all_rows // 2
    square = 2 * rows * edges * width

    head_state = head_state.reshape(1, -1)
    tail_state = tail_state.reshape(1, -1)
    held = {"indices": [head_rows, tail_rows, negatives]}

    def with_(name):
        def hook(got):
            got, held[name] = lax.optimization_barrier((got, held[name]))
            return got

        return hook

    def rotate(x):
        x = lax.ppermute(x, "tail", [(i, (i + i % 2 * 2) % tails) for i in range(tails)])
        return lax.ppermute(x, "tail", [(i, i ^ 1) for i in range(tails)])

    def prepare(got):
        held["prepared"] = call(
            prepare_kernel,
            [
                ((edges, width), BF16),
                ((rows, width), BF16),
                ((2, edges, 128), F32),
                ((2, blocks, rows), F32),
                (head_state.shape, F32),
                (tail_state.shape, F32),
            ],
            0, [], square,
            head_table, tail_table, *held["indices"], head_state, tail_state,
        )
        return with_("prepared")(got)

    gather_hooks = {2: with_("indices"), 1: prepare}
    for k in range(2):
        lo, hi = exchange.all_gather(relations.astype(BF16), gather_hooks)
        if k == 0:
            head_vecs, tail_vecs, tail_col, counts, head_state, tail_state = held["prepared"]
        else:
            tail_vecs = held["tail"]
        keep, send, weights, projected, edge_grad = call(
            functools.partial(score_kernel, k, own, float(nneg)),
            [
                ((half, width), BF16),
                ((half, width), BF16),
                ((edges, rows), BF16),
                ((edges, width), BF16),
                ((edges, width), BF16),
            ],
            3, [pltpu.VMEM((all_rows, width), BF16), pltpu.VMEM((all_rows, width), F32)], 5 * square,
            nat, block_counts, relation_ids, lo, hi, head_vecs, tail_vecs, tail_col, counts,
        )
        head_outs = [(head_table.shape, F32)]
        if k == 0:
            (tail_new,) = call(
                tail_kernel, [((rows + PACK_ROWS, width), BF16)], 0, [], square,
                weights, projected, tail_table, tail_state,
            )
            head_outs += [(head_state.shape, F32), ((edges, width), BF16)]
        else:
            (tail_new,) = call(
                last_tail_kernel, [((rows, width), F32)], 0, [], square,
                weights, projected, tail_vecs,
            )
        head_new = call(
            functools.partial(head_kernel, k, own, blocks), head_outs,
            2, [pltpu.VMEM((all_rows, width), BF16)], 4 * square,
            nat, relation_ids, lo, hi, edge_grad, head_rows, head_table, head_state,
        )
        held["head"] = head_new
        if k == 0:
            held["tail"] = rotate(tail_new)
            grad = exchange.reduce_scatter(keep, send, {1: with_("head")})
            head_table, head_state, head_vecs = held["head"]
            gather_hooks = {1: with_("tail")}
        else:
            held["tail"] = tail_new
            first, second = with_("tail"), with_("head")
            grad = exchange.reduce_scatter(keep, send, {1: lambda got: second(first(got))})
        relation_state = relation_state + grad * grad
        relations = relations - RATE_RELATIONS * grad / (jnp.sqrt(relation_state) + EPSILON)
    return (held["head"][0], held["tail"], relations)


def solution(mesh):
    both = P(AXES, None)
    in_specs = (
        both,
        P(AXES),
        both,
        P(AXES),
        both,
        both,
        P(None, AXES),
        P(None, AXES),
        P(None, AXES, None),
        P(None, AXES),
        P(None, AXES),
    )
    return jax.shard_map(
        shards, mesh=mesh, in_specs=in_specs, out_specs=(both, both, both), check_vma=False
    )
```

```python
import functools

import jax
import jax.numpy as jnp
import numpy as np
from jax import lax
from jax.experimental import pallas as pl
from jax.experimental.pallas import tpu as pltpu
from jax.sharding import PartitionSpec as P

RATE_ROWS = 0.2
RATE_RELATIONS = 0.05
EPSILON = 1e-06
AXES = ("head", "tail")
F32, BF16 = jnp.float32, jnp.bfloat16
ROWS, COLS = 0, 1
PACK_ROWS = 16
VMEM_LIMIT = 24 * 1024 * 1024
VMEM = pl.BlockSpec(memory_space=pltpu.VMEM)
SMEM = pl.BlockSpec(memory_space=pltpu.SMEM)


def dot(a, b, contract_a, contract_b):
    return lax.dot_general(
        a, b, (((contract_a,), (contract_b,)), ((), ())), preferred_element_type=F32
    )


def to_column(row):
    return jnp.broadcast_to(row, (128, row.shape[1])).T


def spread(column, width):
    return jnp.concatenate([column] * (width // column.shape[1]), axis=1)


def adagrad_rows(table, state_row, gradient):
    width = gradient.shape[1]
    mean = jnp.sum(gradient * gradient, axis=1, keepdims=True) * (1.0 / width)
    state = to_column(state_row) + mean
    factor = RATE_ROWS / (jnp.sqrt(state) + EPSILON)
    return table - gradient * spread(factor, width), state


def one_hot_rows(index_row, rows):
    n = index_row.shape[1]
    return (lax.broadcasted_iota(jnp.int32, (rows, n), 0) == index_row).astype(F32).astype(BF16)


def restore_relations(nat_ref, lo_ref, hi_ref, rel_s, own):
    half = lo_ref.shape[0]
    if own % PACK_ROWS:
        rel_s[:half] = lo_ref[...]
        rel_s[half:] = hi_ref[...]
        return
    for part, ref in enumerate((lo_ref, hi_ref)):
        for j in range(half // own):
            block = nat_ref[part * (half // own) + j]
            rel_s[pl.ds(pl.multiple_of(block * own, own), own)] = ref[j * own : (j + 1) * own]


def prepare_kernel(
    head_ref, tail_ref, hrows_ref, trows_ref, neg_ref, hstate_ref, tstate_ref,
    h_ref, t_ref, tcol_ref, cnt_ref, hstate_out_ref, tstate_out_ref,
):
    hstate_out_ref[...] = hstate_ref[...]
    tstate_out_ref[...] = tstate_ref[...]
    buckets = hrows_ref.shape[0]
    blocks, nneg = neg_ref.shape[1:]
    pick = one_hot_rows(hrows_ref[0:1, :], head_ref.shape[0])
    h_ref[...] = dot(pick, head_ref[...].astype(BF16), ROWS, ROWS).astype(BF16)
    t_ref[...] = tail_ref[...].astype(BF16)
    ones = jnp.ones((8, nneg), BF16)
    for k in range(buckets):
        tcol_ref[k] = to_column(trows_ref[k : k + 1, :].astype(F32))
        for b in range(blocks):
            hot = one_hot_rows(neg_ref[k, b : b + 1, :], tail_ref.shape[0])
            cnt_ref[k, b : b + 1, :] = dot(ones, hot, COLS, COLS)[0:1, :]


def score_kernel(
    k, own, nneg, nat_ref, live_ref, rel_ref, lo_ref, hi_ref, h_ref, t_ref, tcol_ref, cnt_ref,
    keep_ref, send_ref, w_ref, u_ref, gu_ref, rel_s, grad_s,
):
    edges, width = h_ref.shape
    blocks, rows = cnt_ref.shape[1:]
    size = edges // blocks
    relations = rel_s.shape[0] // width
    restore_relations(nat_ref, lo_ref, hi_ref, rel_s, own)
    half = keep_ref.shape[0]
    for b in range(blocks):
        part = slice(b * size, (b + 1) * size)
        chosen = rel_s[pl.ds(pl.multiple_of(rel_ref[k, b] * width, width), width)]
        u_ref[part] = dot(h_ref[part], chosen, COLS, ROWS).astype(BF16)
    tails = t_ref[0:rows]
    score = dot(u_ref[...], tails, COLS, COLS)
    row_id = lax.broadcasted_iota(jnp.int32, (size, rows), 1).astype(F32)
    for b in range(blocks):
        part = slice(b * size, (b + 1) * size)
        half_live = jnp.where(live_ref[k, 0] > b, 0.5, 0.0)
        share = cnt_ref[k, b : b + 1, :] * (half_live / nneg)
        t = jnp.tanh(0.5 * score[part])
        is_tail = spread(tcol_ref[k, part], rows) == row_id
        weight = (share + share * t) - jnp.where(is_tail, half_live - half_live * t, 0.0)
        w_ref[part] = weight.astype(BF16)
    gu = dot(w_ref[...], tails, COLS, ROWS).astype(BF16)
    gu_ref[...] = gu
    for r in range(relations):
        parts = []
        for b in range(blocks):
            part = h_ref[b * size : (b + 1) * size]
            parts.append(jnp.where(rel_ref[k, b] == r, part, jnp.zeros_like(part)))
        grad_s[r * width : (r + 1) * width] = dot(jnp.concatenate(parts), gu, ROWS, ROWS).astype(BF16)
    if own % PACK_ROWS:
        keep_ref[...] = grad_s[:half]
        send_ref[...] = grad_s[half:]
        return
    for part, ref in enumerate((keep_ref, send_ref)):
        for j in range(half // own):
            block = nat_ref[part * (half // own) + j]
            rows_of = pl.ds(pl.multiple_of(block * own, own), own)
            ref[j * own : (j + 1) * own] = grad_s[rows_of]


def tail_kernel(w_ref, u_ref, table_ref, state_ref, out_ref):
    rows, width = table_ref.shape
    gradient = dot(w_ref[...], u_ref[...], ROWS, ROWS)
    table, state = adagrad_rows(table_ref[...], state_ref[...], gradient)
    out_ref[0:rows] = table.astype(BF16)
    state_row = state.T[0:1, :]
    high = state_row.astype(BF16).astype(F32)
    row_id = lax.broadcasted_iota(jnp.int32, (PACK_ROWS, width), 0)
    packed = jnp.where(row_id == 0, high, jnp.where(row_id == 1, state_row - high, 0.0))
    out_ref[rows : rows + PACK_ROWS] = packed.astype(BF16)


def last_tail_kernel(w_ref, u_ref, packed_ref, out_ref):
    rows = out_ref.shape[0]
    gradient = dot(w_ref[...], u_ref[...], ROWS, ROWS)
    packed = packed_ref[rows : rows + PACK_ROWS].astype(F32)
    state_row = packed[0:1, :] + packed[1:2, :]
    out_ref[...] = adagrad_rows(packed_ref[0:rows].astype(F32), state_row, gradient)[0]


def head_kernel(
    k, own, blocks, nat_ref, rel_ref, lo_ref, hi_ref, gu_ref, hrows_ref, table_ref, state_ref, *rest
):
    out_ref, rel_s = rest[0], rest[-1]
    rows, width = table_ref.shape
    restore_relations(nat_ref, lo_ref, hi_ref, rel_s, own)
    size = gu_ref.shape[0] // blocks
    terms = []
    for b in range(blocks):
        chosen = rel_s[pl.ds(pl.multiple_of(rel_ref[k, b] * width, width), width)]
        terms.append(dot(gu_ref[b * size : (b + 1) * size], chosen, COLS, COLS).astype(BF16))
    hot = one_hot_rows(hrows_ref[k : k + 1, :], rows)
    gradient = dot(hot, jnp.concatenate(terms), COLS, ROWS)
    table, state = adagrad_rows(table_ref[...], state_ref[...], gradient)
    out_ref[...] = table
    if len(rest) > 2:
        state_out_ref, h_ref = rest[1:3]
        state_out_ref[...] = state.T[0:1, :]
        pick = one_hot_rows(hrows_ref[k + 1 : k + 2, :], rows)
        h_ref[...] = dot(pick, table.astype(BF16), ROWS, ROWS).astype(BF16)


def call(kernel, outs, smem, scratch, flops, *args):
    outs = [jax.ShapeDtypeStruct(shape, kind) for shape, kind in outs]
    moved = sum(a.size * a.dtype.itemsize for a in (*args, *outs))
    return pl.pallas_call(
        kernel,
        out_shape=outs,
        in_specs=[SMEM] * smem + [VMEM] * (len(args) - smem),
        out_specs=[VMEM] * len(outs),
        scratch_shapes=scratch,
        compiler_params=pltpu.CompilerParams(vmem_limit_bytes=VMEM_LIMIT),
        cost_estimate=pl.CostEstimate(flops=flops, bytes_accessed=moved, transcendentals=0),
    )(*args)


class Exchange:
    def __init__(self, heads, tails):
        self.devices = heads * tails
        head_bits = [tails << i for i in range(heads.bit_length() - 1)]
        tail_bits = [1 << i for i in range(tails.bit_length() - 1)]
        rest = head_bits[1:2] + tail_bits + head_bits[2:]
        pairs = [rest[i : i + 2] for i in range(0, len(rest), 2)]
        self.stages = [head_bits[:1]] + pairs
        bits = head_bits[:1] + rest
        places = [self.others(bits, j) for j in range(self.devices)]
        slots = np.zeros(self.devices, np.int32)
        slots[places] = np.arange(self.devices)
        me = lax.axis_index(AXES)
        self.block_of_slot = jnp.asarray(places, jnp.int32) ^ me
        self.slot_of_block = jnp.asarray(slots)[jnp.arange(self.devices, dtype=jnp.int32) ^ me]

    def others(self, bits, j):
        return sum(bit for i, bit in enumerate(bits) if j >> (len(bits) - 1 - i) & 1)

    def masks(self, stage):
        return [self.others(stage, j) for j in range(1, 1 << len(stage))]

    def swap(self, x, mask):
        return lax.ppermute(x, AXES, [(i, i ^ mask) for i in range(self.devices)])

    def reduce_scatter(self, keep, send, hooks):
        if (2 * keep.shape[0] // self.devices) % PACK_ROWS:
            both = jnp.concatenate([keep, send])
            both = both.reshape(self.devices, -1, both.shape[1])[self.block_of_slot]
            keep, send = jnp.split(both.reshape(-1, both.shape[2]), 2)
        parts = [keep, send]
        for i, stage in enumerate(self.stages):
            got = [self.swap(part, mask) for part, mask in zip(parts[1:], self.masks(stage))]
            pieces = parts[:1] + hooks.get(i, list)(got)
            if i + 1 == len(self.stages):
                return sum(piece.astype(F32) for piece in pieces)
            count = 1 << len(self.stages[i + 1])
            size = pieces[0].shape[0] // count
            parts = [
                sum(piece[j * size : (j + 1) * size].astype(F32) for piece in pieces).astype(BF16)
                for j in range(count)
            ]

    def all_gather(self, own, hooks):
        rows = own.shape[0]
        for i, stage in reversed(list(enumerate(self.stages))[1:]):
            got = [self.swap(own, mask) for mask in self.masks(stage)]
            own = jnp.concatenate([own] + hooks.get(i, list)(got))
        lo, hi = own, self.swap(own, self.masks(self.stages[0])[0])
        if rows % PACK_ROWS:
            both = jnp.concatenate([lo, hi]).reshape(self.devices, rows, -1)[self.slot_of_block]
            lo, hi = jnp.split(both.reshape(self.devices * rows, -1), 2)
        return lo, hi


def shards(
    head_table,
    head_state,
    tail_table,
    tail_state,
    relations,
    relation_state,
    head_rows,
    tail_rows,
    negatives,
    relation_ids,
    block_counts,
):
    heads, tails = lax.axis_size("head"), lax.axis_size("tail")
    exchange = Exchange(heads, tails)
    nat = exchange.block_of_slot
    own = relations.shape[0]
    rows, width = tail_table.shape
    edges = head_rows.shape[1]
    blocks, nneg = negatives.shape[1:]
    all_rows = relations.shape[0] * exchange.devices
    half = all_rows // 2
    square = 2 * rows * edges * width

    head_state = head_state.reshape(1, -1)
    tail_state = tail_state.reshape(1, -1)
    held = {"indices": [head_rows, tail_rows, negatives]}

    def with_(name):
        def hook(got):
            got, held[name] = lax.optimization_barrier((got, held[name]))
            return got

        return hook

    def rotate(x):
        x = lax.ppermute(x, "tail", [(i, (i + i % 2 * 2) % tails) for i in range(tails)])
        return lax.ppermute(x, "tail", [(i, i ^ 1) for i in range(tails)])

    def prepare(got):
        held["prepared"] = call(
            prepare_kernel,
            [
                ((edges, width), BF16),
                ((rows, width), BF16),
                ((2, edges, 128), F32),
                ((2, blocks, rows), F32),
                (head_state.shape, F32),
                (tail_state.shape, F32),
            ],
            0, [], square,
            head_table, tail_table, *held["indices"], head_state, tail_state,
        )
        return with_("prepared")(got)

    gather_hooks = {2: with_("indices"), 1: prepare}
    for k in range(2):
        lo, hi = exchange.all_gather(relations.astype(BF16), gather_hooks)
        if k == 0:
            head_vecs, tail_vecs, tail_col, counts, head_state, tail_state = held["prepared"]
        else:
            tail_vecs = held["tail"]
        keep, send, weights, projected, edge_grad = call(
            functools.partial(score_kernel, k, own, float(nneg)),
            [
                ((half, width), BF16),
                ((half, width), BF16),
                ((edges, rows), BF16),
                ((edges, width), BF16),
                ((edges, width), BF16),
            ],
            3, [pltpu.VMEM((all_rows, width), BF16), pltpu.VMEM((all_rows, width), BF16)], 5 * square,
            nat, block_counts, relation_ids, lo, hi, head_vecs, tail_vecs, tail_col, counts,
        )
        head_outs = [(head_table.shape, F32)]
        if k == 0:
            (tail_new,) = call(
                tail_kernel, [((rows + PACK_ROWS, width), BF16)], 0, [], square,
                weights, projected, tail_table, tail_state,
            )
            head_outs += [(head_state.shape, F32), ((edges, width), BF16)]
        else:
            (tail_new,) = call(
                last_tail_kernel, [((rows, width), F32)], 0, [], square,
                weights, projected, tail_vecs,
            )
        head_new = call(
            functools.partial(head_kernel, k, own, blocks), head_outs,
            2, [pltpu.VMEM((all_rows, width), BF16)], 4 * square,
            nat, relation_ids, lo, hi, edge_grad, head_rows, head_table, head_state,
        )
        held["head"] = head_new
        if k == 0:
            held["tail"] = rotate(tail_new)
            grad = exchange.reduce_scatter(keep, send, {1: with_("head")})
            head_table, head_state, head_vecs = held["head"]
            gather_hooks = {1: with_("tail")}
        else:
            held["tail"] = tail_new
            grad = exchange.reduce_scatter(keep, send, {1: with_("head"), 2: with_("tail")})
        relation_state = relation_state + grad * grad
        relations = relations - RATE_RELATIONS * grad / (jnp.sqrt(relation_state) + EPSILON)
    return (held["head"][0], held["tail"], relations)


def solution(mesh):
    both = P(AXES, None)
    in_specs = (
        both,
        P(AXES),
        both,
        P(AXES),
        both,
        both,
        P(None, AXES),
        P(None, AXES),
        P(None, AXES, None),
        P(None, AXES),
        P(None, AXES),
    )
    return jax.shard_map(
        shards, mesh=mesh, in_specs=in_specs, out_specs=(both, both, both), check_vma=False
    )
```

```python
import functools

import jax
import jax.numpy as jnp
import numpy as np
from jax import lax
from jax.experimental import pallas as pl
from jax.experimental.pallas import tpu as pltpu
from jax.sharding import PartitionSpec as P

RATE_ROWS = 0.2
RATE_RELATIONS = 0.05
EPSILON = 1e-06
AXES = ("head", "tail")
F32, BF16 = jnp.float32, jnp.bfloat16
ROWS, COLS = 0, 1
PACK_ROWS = 16
VMEM_LIMIT = 24 * 1024 * 1024
VMEM = pl.BlockSpec(memory_space=pltpu.VMEM)
SMEM = pl.BlockSpec(memory_space=pltpu.SMEM)


def dot(a, b, contract_a, contract_b):
    return lax.dot_general(
        a, b, (((contract_a,), (contract_b,)), ((), ())), preferred_element_type=F32
    )


def to_column(row):
    return jnp.broadcast_to(row, (128, row.shape[1])).T


def spread(column, width):
    return jnp.concatenate([column] * (width // column.shape[1]), axis=1)


def adagrad_rows(table, state_row, gradient):
    width = gradient.shape[1]
    mean = jnp.sum(gradient * gradient, axis=1, keepdims=True) * (1.0 / width)
    state = to_column(state_row) + mean
    factor = RATE_ROWS / (jnp.sqrt(state) + EPSILON)
    return table - gradient * spread(factor, width), state


def one_hot_rows(index_row, rows):
    n = index_row.shape[1]
    return (lax.broadcasted_iota(jnp.int32, (rows, n), 0) == index_row).astype(F32).astype(BF16)


def restore_relations(nat_ref, lo_ref, hi_ref, rel_s, own):
    half = lo_ref.shape[0]
    if own % PACK_ROWS:
        rel_s[:half] = lo_ref[...]
        rel_s[half:] = hi_ref[...]
        return
    for part, ref in enumerate((lo_ref, hi_ref)):
        for j in range(half // own):
            block = nat_ref[part * (half // own) + j]
            rel_s[pl.ds(pl.multiple_of(block * own, own), own)] = ref[j * own : (j + 1) * own]


def prepare_kernel(
    head_ref, tail_ref, hrows_ref, trows_ref, neg_ref, hstate_ref, tstate_ref,
    h_ref, t_ref, tcol_ref, cnt_ref, hstate_out_ref, tstate_out_ref,
):
    hstate_out_ref[...] = hstate_ref[...]
    tstate_out_ref[...] = tstate_ref[...]
    buckets = hrows_ref.shape[0]
    blocks, nneg = neg_ref.shape[1:]
    pick = one_hot_rows(hrows_ref[0:1, :], head_ref.shape[0])
    h_ref[...] = dot(pick, head_ref[...].astype(BF16), ROWS, ROWS).astype(BF16)
    t_ref[...] = tail_ref[...].astype(BF16)
    ones = jnp.ones((8, nneg), BF16)
    for k in range(buckets):
        tcol_ref[k] = to_column(trows_ref[k : k + 1, :].astype(F32))
        for b in range(blocks):
            hot = one_hot_rows(neg_ref[k, b : b + 1, :], tail_ref.shape[0])
            cnt_ref[k, b : b + 1, :] = dot(ones, hot, COLS, COLS)[0:1, :]


def score_kernel(
    k, own, nneg, cuts, nat_ref, live_ref, rel_ref, lo_ref, hi_ref, h_ref, t_ref, tcol_ref, cnt_ref,
    w_ref, u_ref, gu_ref, *rest,
):
    grad_refs, (rel_s, grad_s) = rest[:cuts], rest[cuts:]
    edges, width = h_ref.shape
    blocks, rows = cnt_ref.shape[1:]
    size = edges // blocks
    relations = rel_s.shape[0] // width
    restore_relations(nat_ref, lo_ref, hi_ref, rel_s, own)
    for b in range(blocks):
        part = slice(b * size, (b + 1) * size)
        chosen = rel_s[pl.ds(pl.multiple_of(rel_ref[k, b] * width, width), width)]
        u_ref[part] = dot(h_ref[part], chosen, COLS, ROWS).astype(BF16)
    tails = t_ref[0:rows]
    score = dot(u_ref[...], tails, COLS, COLS)
    row_id = lax.broadcasted_iota(jnp.int32, (size, rows), 1).astype(F32)
    for b in range(blocks):
        part = slice(b * size, (b + 1) * size)
        half_live = jnp.where(live_ref[k, 0] > b, 0.5, 0.0)
        share = cnt_ref[k, b : b + 1, :] * (half_live / nneg)
        t = jnp.tanh(0.5 * score[part])
        is_tail = spread(tcol_ref[k, part], rows) == row_id
        weight = (share + share * t) - jnp.where(is_tail, half_live - half_live * t, 0.0)
        w_ref[part] = weight.astype(BF16)
    gu = dot(w_ref[...], tails, COLS, ROWS).astype(BF16)
    gu_ref[...] = gu
    for r in range(relations):
        parts = []
        for b in range(blocks):
            part = h_ref[b * size : (b + 1) * size]
            parts.append(jnp.where(rel_ref[k, b] == r, part, jnp.zeros_like(part)))
        grad_s[r * width : (r + 1) * width] = dot(jnp.concatenate(parts), gu, ROWS, ROWS).astype(BF16)
    for i, ref in enumerate(grad_refs):
        count = ref.shape[0]
        if own % PACK_ROWS:
            ref[...] = grad_s[i * count : (i + 1) * count]
            continue
        for j in range(count // own):
            block = nat_ref[i * (count // own) + j]
            ref[j * own : (j + 1) * own] = grad_s[pl.ds(pl.multiple_of(block * own, own), own)]


def tail_kernel(w_ref, u_ref, table_ref, state_ref, out_ref):
    rows, width = table_ref.shape
    gradient = dot(w_ref[...], u_ref[...], ROWS, ROWS)
    table, state = adagrad_rows(table_ref[...], state_ref[...], gradient)
    out_ref[0:rows] = table.astype(BF16)
    state_row = state.T[0:1, :]
    high = state_row.astype(BF16).astype(F32)
    row_id = lax.broadcasted_iota(jnp.int32, (PACK_ROWS, width), 0)
    packed = jnp.where(row_id == 0, high, jnp.where(row_id == 1, state_row - high, 0.0))
    out_ref[rows : rows + PACK_ROWS] = packed.astype(BF16)


def last_tail_kernel(w_ref, u_ref, packed_ref, out_ref):
    rows = out_ref.shape[0]
    gradient = dot(w_ref[...], u_ref[...], ROWS, ROWS)
    packed = packed_ref[rows : rows + PACK_ROWS].astype(F32)
    state_row = packed[0:1, :] + packed[1:2, :]
    out_ref[...] = adagrad_rows(packed_ref[0:rows].astype(F32), state_row, gradient)[0]


def head_kernel(
    k, own, blocks, nat_ref, rel_ref, lo_ref, hi_ref, gu_ref, hrows_ref, table_ref, state_ref, *rest
):
    out_ref, rel_s = rest[0], rest[-1]
    rows, width = table_ref.shape
    restore_relations(nat_ref, lo_ref, hi_ref, rel_s, own)
    size = gu_ref.shape[0] // blocks
    terms = []
    for b in range(blocks):
        chosen = rel_s[pl.ds(pl.multiple_of(rel_ref[k, b] * width, width), width)]
        terms.append(dot(gu_ref[b * size : (b + 1) * size], chosen, COLS, COLS).astype(BF16))
    hot = one_hot_rows(hrows_ref[k : k + 1, :], rows)
    gradient = dot(hot, jnp.concatenate(terms), COLS, ROWS)
    table, state = adagrad_rows(table_ref[...], state_ref[...], gradient)
    out_ref[...] = table
    if len(rest) > 2:
        state_out_ref, h_ref = rest[1:3]
        state_out_ref[...] = state.T[0:1, :]
        pick = one_hot_rows(hrows_ref[k + 1 : k + 2, :], rows)
        h_ref[...] = dot(pick, table.astype(BF16), ROWS, ROWS).astype(BF16)


def call(kernel, outs, smem, scratch, flops, *args):
    outs = [jax.ShapeDtypeStruct(shape, kind) for shape, kind in outs]
    moved = sum(a.size * a.dtype.itemsize for a in (*args, *outs))
    return pl.pallas_call(
        kernel,
        out_shape=outs,
        in_specs=[SMEM] * smem + [VMEM] * (len(args) - smem),
        out_specs=[VMEM] * len(outs),
        scratch_shapes=scratch,
        compiler_params=pltpu.CompilerParams(vmem_limit_bytes=VMEM_LIMIT),
        cost_estimate=pl.CostEstimate(flops=flops, bytes_accessed=moved, transcendentals=0),
    )(*args)


class Exchange:
    def __init__(self, heads, tails):
        self.devices = heads * tails
        head_bits = [tails << i for i in range(heads.bit_length() - 1)]
        tail_bits = [1 << i for i in range(tails.bit_length() - 1)]
        rest = head_bits[1:2] + tail_bits + head_bits[2:]
        pairs = [rest[i : i + 2] for i in range(0, len(rest), 2)]
        self.stages = [head_bits[:1]] + pairs
        bits = head_bits[:1] + rest
        places = [self.others(bits, j) for j in range(self.devices)]
        slots = np.zeros(self.devices, np.int32)
        slots[places] = np.arange(self.devices)
        me = lax.axis_index(AXES)
        self.block_of_slot = jnp.asarray(places, jnp.int32) ^ me
        self.slot_of_block = jnp.asarray(slots)[jnp.arange(self.devices, dtype=jnp.int32) ^ me]

    def others(self, bits, j):
        return sum(bit for i, bit in enumerate(bits) if j >> (len(bits) - 1 - i) & 1)

    def masks(self, stage):
        return [self.others(stage, j) for j in range(1, 1 << len(stage))]

    def swap(self, x, mask):
        return lax.ppermute(x, AXES, [(i, i ^ mask) for i in range(self.devices)])

    def reduce_scatter(self, parts, hooks):
        if sum(part.shape[0] for part in parts) // self.devices % PACK_ROWS:
            both = jnp.concatenate(parts)
            both = both.reshape(self.devices, -1, both.shape[1])[self.block_of_slot]
            parts = jnp.split(both.reshape(-1, both.shape[2]), len(parts))
        if len(parts) > 2:
            half = len(parts) // 2
            mask = self.masks(self.stages[0])[0]
            got = [self.swap(part, mask) for part in parts[half:]]
            parts = [(a.astype(F32) + b.astype(F32)).astype(BF16) for a, b in zip(parts[:half], got)]
            parts[0] = hooks["own"](parts[0])
        for i, stage in enumerate(self.stages):
            if len(parts) != 1 << len(stage):
                continue
            got = [self.swap(part, mask) for part, mask in zip(parts[1:], self.masks(stage))]
            pieces = parts[:1] + hooks.get(i, list)(got)
            if i + 1 == len(self.stages):
                return sum(piece.astype(F32) for piece in pieces)
            count = 1 << len(self.stages[i + 1])
            size = pieces[0].shape[0] // count
            parts = [
                sum(piece[j * size : (j + 1) * size].astype(F32) for piece in pieces).astype(BF16)
                for j in range(count)
            ]

    def all_gather(self, own, hooks):
        rows = own.shape[0]
        for i, stage in reversed(list(enumerate(self.stages))[1:]):
            got = [self.swap(own, mask) for mask in self.masks(stage)]
            own = jnp.concatenate([own] + hooks.get(i, list)(got))
        lo, hi = own, self.swap(own, self.masks(self.stages[0])[0])
        if rows % PACK_ROWS:
            both = jnp.concatenate([lo, hi]).reshape(self.devices, rows, -1)[self.slot_of_block]
            lo, hi = jnp.split(both.reshape(self.devices * rows, -1), 2)
        return lo, hi


def shards(
    head_table,
    head_state,
    tail_table,
    tail_state,
    relations,
    relation_state,
    head_rows,
    tail_rows,
    negatives,
    relation_ids,
    block_counts,
):
    heads, tails = lax.axis_size("head"), lax.axis_size("tail")
    exchange = Exchange(heads, tails)
    nat = exchange.block_of_slot
    own = relations.shape[0]
    rows, width = tail_table.shape
    edges = head_rows.shape[1]
    blocks, nneg = negatives.shape[1:]
    all_rows = relations.shape[0] * exchange.devices
    half = all_rows // 2
    square = 2 * rows * edges * width

    head_state = head_state.reshape(1, -1)
    tail_state = tail_state.reshape(1, -1)
    held = {"indices": [head_rows, tail_rows, negatives]}

    def with_(name):
        def hook(got):
            got, held[name] = lax.optimization_barrier((got, held[name]))
            return got

        return hook

    def rotate(x):
        x = lax.ppermute(x, "tail", [(i, (i + i % 2 * 2) % tails) for i in range(tails)])
        return lax.ppermute(x, "tail", [(i, i ^ 1) for i in range(tails)])

    def prepare(got):
        held["prepared"] = call(
            prepare_kernel,
            [
                ((edges, width), BF16),
                ((rows, width), BF16),
                ((2, edges, 128), F32),
                ((2, blocks, rows), F32),
                (head_state.shape, F32),
                (tail_state.shape, F32),
            ],
            0, [], square,
            head_table, tail_table, *held["indices"], head_state, tail_state,
        )
        return with_("prepared")(got)

    gather_hooks = {2: with_("indices"), 1: prepare}
    for k in range(2):
        lo, hi = exchange.all_gather(relations.astype(BF16), gather_hooks)
        if k == 0:
            head_vecs, tail_vecs, tail_col, counts, head_state, tail_state = held["prepared"]
        else:
            tail_vecs = held["tail"]
        cuts = 2 if k == 0 else 2 << len(exchange.stages[1])
        weights, projected, edge_grad, *terms = call(
            functools.partial(score_kernel, k, own, float(nneg), cuts),
            [((edges, rows), BF16), ((edges, width), BF16), ((edges, width), BF16)]
            + [((all_rows // cuts, width), BF16)] * cuts,
            3, [pltpu.VMEM((all_rows, width), BF16), pltpu.VMEM((all_rows, width), BF16)], 5 * square,
            nat, block_counts, relation_ids, lo, hi, head_vecs, tail_vecs, tail_col, counts,
        )

        def update_heads(edge_grad, outs):
            return call(
                functools.partial(head_kernel, k, own, blocks), [(head_table.shape, F32), *outs],
                2, [pltpu.VMEM((all_rows, width), BF16)], 4 * square,
                nat, relation_ids, lo, hi, edge_grad, head_rows, head_table, head_state,
            )

        if k == 0:
            (tail_new,) = call(
                tail_kernel, [((rows + PACK_ROWS, width), BF16)], 0, [], square,
                weights, projected, tail_table, tail_state,
            )
            held["tail"] = rotate(tail_new)
            held["head"] = update_heads(edge_grad, [(head_state.shape, F32), ((edges, width), BF16)])
            grad = exchange.reduce_scatter(terms, {1: with_("head")})
            head_table, head_state, head_vecs = held["head"]
            gather_hooks = {1: with_("tail")}
        else:

            def last_updates(part):
                part, ready = lax.optimization_barrier((part, [weights, projected, edge_grad]))
                held["tail"] = call(
                    last_tail_kernel, [((rows, width), F32)], 0, [], square, *ready[:2], tail_vecs
                )
                held["head"] = update_heads(ready[2], [])
                return part

            hooks = {"own": last_updates, 1: lambda got: with_("head")(got[::-1])[::-1], 2: with_("tail")}
            grad = exchange.reduce_scatter(terms, hooks)
        relation_state = relation_state + grad * grad
        relations = relations - RATE_RELATIONS * grad / (jnp.sqrt(relation_state) + EPSILON)
    return (held["head"][0], held["tail"][0], relations)


def solution(mesh):
    both = P(AXES, None)
    in_specs = (
        both,
        P(AXES),
        both,
        P(AXES),
        both,
        both,
        P(None, AXES),
        P(None, AXES),
        P(None, AXES, None),
        P(None, AXES),
        P(None, AXES),
    )
    return jax.shard_map(
        shards, mesh=mesh, in_specs=in_specs, out_specs=(both, both, both), check_vma=False
    )
```

```python
import functools

import jax
import jax.numpy as jnp
import numpy as np
from jax import lax
from jax.experimental import pallas as pl
from jax.experimental.pallas import tpu as pltpu
from jax.sharding import PartitionSpec as P

RATE_ROWS = 0.2
RATE_RELATIONS = 0.05
EPSILON = 1e-06
AXES = ("head", "tail")
F32, BF16 = jnp.float32, jnp.bfloat16
ROWS, COLS = 0, 1
PACK_ROWS = 16
VMEM_LIMIT = 24 * 1024 * 1024
VMEM = pl.BlockSpec(memory_space=pltpu.VMEM)
SMEM = pl.BlockSpec(memory_space=pltpu.SMEM)


def dot(a, b, contract_a, contract_b):
    return lax.dot_general(
        a, b, (((contract_a,), (contract_b,)), ((), ())), preferred_element_type=F32
    )


def to_column(row):
    return jnp.broadcast_to(row, (128, row.shape[1])).T


def spread(column, width):
    return jnp.concatenate([column] * (width // column.shape[1]), axis=1)


def adagrad_rows(table, state_row, gradient):
    width = gradient.shape[1]
    mean = jnp.sum(gradient * gradient, axis=1, keepdims=True) * (1.0 / width)
    state = to_column(state_row) + mean
    factor = RATE_ROWS / (jnp.sqrt(state) + EPSILON)
    return table - gradient * spread(factor, width), state


def one_hot_rows(index_row, rows):
    n = index_row.shape[1]
    return (lax.broadcasted_iota(jnp.int32, (rows, n), 0) == index_row).astype(F32).astype(BF16)


def restore_relations(nat_ref, lo_ref, hi_ref, rel_s, own):
    half = lo_ref.shape[0]
    if own % PACK_ROWS:
        rel_s[:half] = lo_ref[...]
        rel_s[half:] = hi_ref[...]
        return
    for part, ref in enumerate((lo_ref, hi_ref)):
        for j in range(half // own):
            block = nat_ref[part * (half // own) + j]
            rel_s[pl.ds(pl.multiple_of(block * own, own), own)] = ref[j * own : (j + 1) * own]


def prepare_kernel(
    head_ref, tail_ref, hrows_ref, trows_ref, neg_ref, hstate_ref, tstate_ref, rel_ref, live_ref,
    h_ref, t_ref, tcol_ref, cnt_ref, hstate_out_ref, tstate_out_ref, rel_out_ref, live_out_ref,
):
    hstate_out_ref[...] = hstate_ref[...]
    tstate_out_ref[...] = tstate_ref[...]
    rel_out_ref[...] = rel_ref[...]
    live_out_ref[...] = live_ref[...]
    buckets = hrows_ref.shape[0]
    blocks, nneg = neg_ref.shape[1:]
    pick = one_hot_rows(hrows_ref[0:1, :], head_ref.shape[0])
    h_ref[...] = dot(pick, head_ref[...].astype(BF16), ROWS, ROWS).astype(BF16)
    t_ref[...] = tail_ref[...].astype(BF16)
    ones = jnp.ones((8, nneg), BF16)
    for k in range(buckets):
        tcol_ref[k] = to_column(trows_ref[k : k + 1, :].astype(F32))
        for b in range(blocks):
            hot = one_hot_rows(neg_ref[k, b : b + 1, :], tail_ref.shape[0])
            cnt_ref[k, b : b + 1, :] = dot(ones, hot, COLS, COLS)[0:1, :]


def score_kernel(
    k, own, nneg, cuts, nat_ref, live_ref, rel_ref, lo_ref, hi_ref, h_ref, t_ref, tcol_ref, cnt_ref,
    w_ref, u_ref, gu_ref, *rest,
):
    grad_refs, (rel_s, grad_s) = rest[:cuts], rest[cuts:]
    edges, width = h_ref.shape
    blocks, rows = cnt_ref.shape[1:]
    size = edges // blocks
    relations = rel_s.shape[0] // width
    restore_relations(nat_ref, lo_ref, hi_ref, rel_s, own)
    for b in range(blocks):
        part = slice(b * size, (b + 1) * size)
        chosen = rel_s[pl.ds(pl.multiple_of(rel_ref[k, b] * width, width), width)]
        u_ref[part] = dot(h_ref[part], chosen, COLS, ROWS).astype(BF16)
    tails = t_ref[0:rows]
    score = dot(u_ref[...], tails, COLS, COLS)
    row_id = lax.broadcasted_iota(jnp.int32, (size, rows), 1).astype(F32)
    for b in range(blocks):
        part = slice(b * size, (b + 1) * size)
        half_live = jnp.where(live_ref[k, 0] > b, 0.5, 0.0)
        share = cnt_ref[k, b : b + 1, :] * (half_live / nneg)
        t = jnp.tanh(0.5 * score[part])
        is_tail = spread(tcol_ref[k, part], rows) == row_id
        weight = (share + share * t) - jnp.where(is_tail, half_live - half_live * t, 0.0)
        w_ref[part] = weight.astype(BF16)
    gu = dot(w_ref[...], tails, COLS, ROWS).astype(BF16)
    gu_ref[...] = gu
    for r in range(relations):
        parts = []
        for b in range(blocks):
            part = h_ref[b * size : (b + 1) * size]
            parts.append(jnp.where(rel_ref[k, b] == r, part, jnp.zeros_like(part)))
        grad_s[r * width : (r + 1) * width] = dot(jnp.concatenate(parts), gu, ROWS, ROWS).astype(BF16)
    for i, ref in enumerate(grad_refs):
        count = ref.shape[0]
        if own % PACK_ROWS:
            ref[...] = grad_s[i * count : (i + 1) * count]
            continue
        for j in range(count // own):
            block = nat_ref[i * (count // own) + j]
            ref[j * own : (j + 1) * own] = grad_s[pl.ds(pl.multiple_of(block * own, own), own)]


def tail_kernel(w_ref, u_ref, table_ref, state_ref, out_ref):
    rows, width = table_ref.shape
    gradient = dot(w_ref[...], u_ref[...], ROWS, ROWS)
    table, state = adagrad_rows(table_ref[...], state_ref[...], gradient)
    out_ref[0:rows] = table.astype(BF16)
    state_row = state.T[0:1, :]
    high = state_row.astype(BF16).astype(F32)
    row_id = lax.broadcasted_iota(jnp.int32, (PACK_ROWS, width), 0)
    packed = jnp.where(row_id == 0, high, jnp.where(row_id == 1, state_row - high, 0.0))
    out_ref[rows : rows + PACK_ROWS] = packed.astype(BF16)


def last_tail_kernel(w_ref, u_ref, packed_ref, out_ref):
    rows = out_ref.shape[0]
    gradient = dot(w_ref[...], u_ref[...], ROWS, ROWS)
    packed = packed_ref[rows : rows + PACK_ROWS].astype(F32)
    state_row = packed[0:1, :] + packed[1:2, :]
    out_ref[...] = adagrad_rows(packed_ref[0:rows].astype(F32), state_row, gradient)[0]


def head_kernel(
    k, own, blocks, nat_ref, rel_ref, lo_ref, hi_ref, gu_ref, hrows_ref, table_ref, state_ref, *rest
):
    out_ref, rel_s = rest[0], rest[-1]
    rows, width = table_ref.shape
    restore_relations(nat_ref, lo_ref, hi_ref, rel_s, own)
    size = gu_ref.shape[0] // blocks
    terms = []
    for b in range(blocks):
        chosen = rel_s[pl.ds(pl.multiple_of(rel_ref[k, b] * width, width), width)]
        terms.append(dot(gu_ref[b * size : (b + 1) * size], chosen, COLS, COLS).astype(BF16))
    hot = one_hot_rows(hrows_ref[k : k + 1, :], rows)
    gradient = dot(hot, jnp.concatenate(terms), COLS, ROWS)
    table, state = adagrad_rows(table_ref[...], state_ref[...], gradient)
    out_ref[...] = table
    if len(rest) > 2:
        state_out_ref, h_ref = rest[1:3]
        state_out_ref[...] = state.T[0:1, :]
        pick = one_hot_rows(hrows_ref[k + 1 : k + 2, :], rows)
        h_ref[...] = dot(pick, table.astype(BF16), ROWS, ROWS).astype(BF16)


def call(kernel, outs, smem, scratch, flops, *args):
    outs = [jax.ShapeDtypeStruct(shape, kind) for shape, kind in outs]
    moved = sum(a.size * a.dtype.itemsize for a in (*args, *outs))
    return pl.pallas_call(
        kernel,
        out_shape=outs,
        in_specs=[SMEM] * smem + [VMEM] * (len(args) - smem),
        out_specs=[VMEM] * len(outs),
        scratch_shapes=scratch,
        compiler_params=pltpu.CompilerParams(vmem_limit_bytes=VMEM_LIMIT),
        cost_estimate=pl.CostEstimate(flops=flops, bytes_accessed=moved, transcendentals=0),
    )(*args)


class Exchange:
    def __init__(self, heads, tails):
        self.devices = heads * tails
        head_bits = [tails << i for i in range(heads.bit_length() - 1)]
        tail_bits = [1 << i for i in range(tails.bit_length() - 1)]
        rest = head_bits[1:2] + tail_bits + head_bits[2:]
        pairs = [rest[i : i + 2] for i in range(0, len(rest), 2)]
        self.stages = [head_bits[:1]] + pairs
        bits = head_bits[:1] + rest
        places = [self.others(bits, j) for j in range(self.devices)]
        slots = np.zeros(self.devices, np.int32)
        slots[places] = np.arange(self.devices)
        me = lax.axis_index(AXES)
        self.block_of_slot = jnp.asarray(places, jnp.int32) ^ me
        self.slot_of_block = jnp.asarray(slots)[jnp.arange(self.devices, dtype=jnp.int32) ^ me]

    def others(self, bits, j):
        return sum(bit for i, bit in enumerate(bits) if j >> (len(bits) - 1 - i) & 1)

    def masks(self, stage):
        return [self.others(stage, j) for j in range(1, 1 << len(stage))]

    def swap(self, x, mask):
        return lax.ppermute(x, AXES, [(i, i ^ mask) for i in range(self.devices)])

    def reduce_scatter(self, parts, hooks):
        if sum(part.shape[0] for part in parts) // self.devices % PACK_ROWS:
            both = jnp.concatenate(parts)
            both = both.reshape(self.devices, -1, both.shape[1])[self.block_of_slot]
            parts = jnp.split(both.reshape(-1, both.shape[2]), len(parts))
        if len(parts) > 2:
            half = len(parts) // 2
            mask = self.masks(self.stages[0])[0]
            got = [self.swap(part, mask) for part in parts[half:]]
            parts = [(a.astype(F32) + b.astype(F32)).astype(BF16) for a, b in zip(parts[:half], got)]
            parts[0] = hooks["own"](parts[0])
        for i, stage in enumerate(self.stages):
            if len(parts) != 1 << len(stage):
                continue
            got = [self.swap(part, mask) for part, mask in zip(parts[1:], self.masks(stage))]
            pieces = parts[:1] + hooks.get(i, list)(got)
            if i + 1 == len(self.stages):
                return sum(piece.astype(F32) for piece in pieces)
            count = 1 << len(self.stages[i + 1])
            size = pieces[0].shape[0] // count
            parts = [
                sum(piece[j * size : (j + 1) * size].astype(F32) for piece in pieces).astype(BF16)
                for j in range(count)
            ]

    def all_gather(self, own, hooks):
        rows = own.shape[0]
        for i, stage in reversed(list(enumerate(self.stages))[1:]):
            got = [self.swap(own, mask) for mask in self.masks(stage)]
            own = jnp.concatenate([own] + hooks.get(i, list)(got))
        lo, hi = own, self.swap(own, self.masks(self.stages[0])[0])
        if rows % PACK_ROWS:
            both = jnp.concatenate([lo, hi]).reshape(self.devices, rows, -1)[self.slot_of_block]
            lo, hi = jnp.split(both.reshape(self.devices * rows, -1), 2)
        return lo, hi


def shards(
    head_table,
    head_state,
    tail_table,
    tail_state,
    relations,
    relation_state,
    head_rows,
    tail_rows,
    negatives,
    relation_ids,
    block_counts,
):
    heads, tails = lax.axis_size("head"), lax.axis_size("tail")
    exchange = Exchange(heads, tails)
    nat = exchange.block_of_slot
    own = relations.shape[0]
    rows, width = tail_table.shape
    edges = head_rows.shape[1]
    blocks, nneg = negatives.shape[1:]
    all_rows = relations.shape[0] * exchange.devices
    half = all_rows // 2
    square = 2 * rows * edges * width

    head_state = head_state.reshape(1, -1)
    tail_state = tail_state.reshape(1, -1)
    held = {"indices": [head_rows, tail_rows, negatives]}

    def with_(name):
        def hook(got):
            got, held[name] = lax.optimization_barrier((got, held[name]))
            return got

        return hook

    def rotate(x):
        x = lax.ppermute(x, "tail", [(i, (i + i % 2 * 2) % tails) for i in range(tails)])
        return lax.ppermute(x, "tail", [(i, i ^ 1) for i in range(tails)])

    def prepare(got):
        held["prepared"] = call(
            prepare_kernel,
            [
                ((edges, width), BF16),
                ((rows, width), BF16),
                ((2, edges, 128), F32),
                ((2, blocks, rows), F32),
                (head_state.shape, F32),
                (tail_state.shape, F32),
                (relation_ids.shape, jnp.int32),
                (block_counts.shape, jnp.int32),
            ],
            0, [], square,
            head_table, tail_table, *held["indices"], head_state, tail_state, relation_ids, block_counts,
        )
        return with_("prepared")(got)

    gather_hooks = {2: with_("indices"), 1: prepare}
    for k in range(2):
        lo, hi = exchange.all_gather(relations.astype(BF16), gather_hooks)
        if k == 0:
            head_vecs, tail_vecs, tail_col, counts, *small = held["prepared"]
            head_state, tail_state, relation_ids, block_counts = small
        else:
            tail_vecs = held["tail"]
        cuts = 2 if k == 0 else 2 << len(exchange.stages[1])
        weights, projected, edge_grad, *terms = call(
            functools.partial(score_kernel, k, own, float(nneg), cuts),
            [((edges, rows), BF16), ((edges, width), BF16), ((edges, width), BF16)]
            + [((all_rows // cuts, width), BF16)] * cuts,
            3, [pltpu.VMEM((all_rows, width), BF16), pltpu.VMEM((all_rows, width), BF16)], 5 * square,
            nat, block_counts, relation_ids, lo, hi, head_vecs, tail_vecs, tail_col, counts,
        )

        def update_heads(edge_grad, outs):
            return call(
                functools.partial(head_kernel, k, own, blocks), [(head_table.shape, F32), *outs],
                2, [pltpu.VMEM((all_rows, width), BF16)], 4 * square,
                nat, relation_ids, lo, hi, edge_grad, head_rows, head_table, head_state,
            )

        if k == 0:
            (tail_new,) = call(
                tail_kernel, [((rows + PACK_ROWS, width), BF16)], 0, [], square,
                weights, projected, tail_table, tail_state,
            )
            held["tail"] = rotate(tail_new)
            held["head"] = update_heads(edge_grad, [(head_state.shape, F32), ((edges, width), BF16)])
            grad = exchange.reduce_scatter(terms, {1: with_("head")})
            head_table, head_state, head_vecs = held["head"]
            gather_hooks = {1: with_("tail")}
        else:

            def last_updates(part):
                part, ready = lax.optimization_barrier((part, [weights, projected, edge_grad]))
                held["tail"] = call(
                    last_tail_kernel, [((rows, width), F32)], 0, [], square, *ready[:2], tail_vecs
                )
                held["head"] = update_heads(ready[2], [])
                return part

            hooks = {"own": last_updates, 1: lambda got: with_("head")(got[::-1])[::-1], 2: with_("tail")}
            grad = exchange.reduce_scatter(terms, hooks)
        relation_state = relation_state + grad * grad
        relations = relations - RATE_RELATIONS * grad / (jnp.sqrt(relation_state) + EPSILON)
    return (held["head"][0], held["tail"][0], relations)


def solution(mesh):
    both = P(AXES, None)
    in_specs = (
        both,
        P(AXES),
        both,
        P(AXES),
        both,
        both,
        P(None, AXES),
        P(None, AXES),
        P(None, AXES, None),
        P(None, AXES),
        P(None, AXES),
    )
    return jax.shard_map(
        shards, mesh=mesh, in_specs=in_specs, out_specs=(both, both, both), check_vma=False
    )
```

```python
import functools

import jax
import jax.numpy as jnp
import numpy as np
from jax import lax
from jax.experimental import pallas as pl
from jax.experimental.pallas import tpu as pltpu
from jax.sharding import PartitionSpec as P

RATE_ROWS = 0.2
RATE_RELATIONS = 0.05
EPSILON = 1e-06
AXES = ("head", "tail")
F32, BF16 = jnp.float32, jnp.bfloat16
ROWS, COLS = 0, 1
PACK_ROWS = 16
VMEM_LIMIT = 24 * 1024 * 1024
VMEM = pl.BlockSpec(memory_space=pltpu.VMEM)
SMEM = pl.BlockSpec(memory_space=pltpu.SMEM)


def dot(a, b, contract_a, contract_b):
    return lax.dot_general(
        a, b, (((contract_a,), (contract_b,)), ((), ())), preferred_element_type=F32
    )


def to_column(row):
    return jnp.broadcast_to(row, (128, row.shape[1])).T


def spread(column, width):
    return jnp.concatenate([column] * (width // column.shape[1]), axis=1)


def adagrad_rows(table, state_row, gradient):
    width = gradient.shape[1]
    mean = jnp.sum(gradient * gradient, axis=1, keepdims=True) * (1.0 / width)
    state = to_column(state_row) + mean
    factor = RATE_ROWS / (jnp.sqrt(state) + EPSILON)
    return table - gradient * spread(factor, width), state


def one_hot_rows(index_row, rows):
    n = index_row.shape[1]
    return (lax.broadcasted_iota(jnp.int32, (rows, n), 0) == index_row).astype(F32).astype(BF16)


def restore_relations(nat_ref, lo_ref, hi_ref, rel_s, own):
    half = lo_ref.shape[0]
    if own % PACK_ROWS:
        rel_s[:half] = lo_ref[...]
        rel_s[half:] = hi_ref[...]
        return
    for part, ref in enumerate((lo_ref, hi_ref)):
        for j in range(half // own):
            block = nat_ref[part * (half // own) + j]
            rel_s[pl.ds(pl.multiple_of(block * own, own), own)] = ref[j * own : (j + 1) * own]


def prepare_kernel(
    head_ref, tail_ref, hrows_ref, trows_ref, neg_ref, hstate_ref, tstate_ref,
    h_ref, t_ref, tcol_ref, cnt_ref, hstate_out_ref, tstate_out_ref,
):
    hstate_out_ref[...] = hstate_ref[...]
    tstate_out_ref[...] = tstate_ref[...]
    buckets = hrows_ref.shape[0]
    blocks, nneg = neg_ref.shape[1:]
    pick = one_hot_rows(hrows_ref[0:1, :], head_ref.shape[0])
    h_ref[...] = dot(pick, head_ref[...].astype(BF16), ROWS, ROWS).astype(BF16)
    t_ref[...] = tail_ref[...].astype(BF16)
    ones = jnp.ones((8, nneg), BF16)
    for k in range(buckets):
        tcol_ref[k] = to_column(trows_ref[k : k + 1, :].astype(F32))
        for b in range(blocks):
            hot = one_hot_rows(neg_ref[k, b : b + 1, :], tail_ref.shape[0])
            cnt_ref[k, b : b + 1, :] = dot(ones, hot, COLS, COLS)[0:1, :]


def score_kernel(
    k, own, nneg, cuts, nat_ref, live_ref, rel_ref, lo_ref, hi_ref, h_ref, t_ref, tcol_ref, cnt_ref,
    w_ref, u_ref, gu_ref, *rest,
):
    grad_refs, (rel_s, grad_s) = rest[:cuts], rest[cuts:]
    edges, width = h_ref.shape
    blocks, rows = cnt_ref.shape[1:]
    size = edges // blocks
    relations = rel_s.shape[0] // width
    restore_relations(nat_ref, lo_ref, hi_ref, rel_s, own)
    for b in range(blocks):
        part = slice(b * size, (b + 1) * size)
        chosen = rel_s[pl.ds(pl.multiple_of(rel_ref[k, b] * width, width), width)]
        u_ref[part] = dot(h_ref[part], chosen, COLS, ROWS).astype(BF16)
    tails = t_ref[0:rows]
    score = dot(u_ref[...], tails, COLS, COLS)
    row_id = lax.broadcasted_iota(jnp.int32, (size, rows), 1).astype(F32)
    for b in range(blocks):
        part = slice(b * size, (b + 1) * size)
        half_live = jnp.where(live_ref[k, 0] > b, 0.5, 0.0)
        share = cnt_ref[k, b : b + 1, :] * (half_live / nneg)
        t = jnp.tanh(0.5 * score[part])
        is_tail = spread(tcol_ref[k, part], rows) == row_id
        weight = (share + share * t) - jnp.where(is_tail, half_live - half_live * t, 0.0)
        w_ref[part] = weight.astype(BF16)
    gu = dot(w_ref[...], tails, COLS, ROWS).astype(BF16)
    gu_ref[...] = gu
    for r in range(relations):
        parts = []
        for b in range(blocks):
            part = h_ref[b * size : (b + 1) * size]
            parts.append(jnp.where(rel_ref[k, b] == r, part, jnp.zeros_like(part)))
        grad_s[r * width : (r + 1) * width] = dot(jnp.concatenate(parts), gu, ROWS, ROWS).astype(BF16)
    for i, ref in enumerate(grad_refs):
        count = ref.shape[0]
        if own % PACK_ROWS:
            ref[...] = grad_s[i * count : (i + 1) * count]
            continue
        for j in range(count // own):
            block = nat_ref[i * (count // own) + j]
            ref[j * own : (j + 1) * own] = grad_s[pl.ds(pl.multiple_of(block * own, own), own)]


def tail_kernel(w_ref, u_ref, table_ref, state_ref, out_ref):
    rows, width = table_ref.shape
    gradient = dot(w_ref[...], u_ref[...], ROWS, ROWS)
    table, state = adagrad_rows(table_ref[...], state_ref[...], gradient)
    out_ref[0:rows] = table.astype(BF16)
    state_row = state.T[0:1, :]
    high = state_row.astype(BF16).astype(F32)
    row_id = lax.broadcasted_iota(jnp.int32, (PACK_ROWS, width), 0)
    packed = jnp.where(row_id == 0, high, jnp.where(row_id == 1, state_row - high, 0.0))
    out_ref[rows : rows + PACK_ROWS] = packed.astype(BF16)


def last_tail_kernel(w_ref, u_ref, packed_ref, out_ref):
    rows = out_ref.shape[0]
    gradient = dot(w_ref[...], u_ref[...], ROWS, ROWS)
    packed = packed_ref[rows : rows + PACK_ROWS].astype(F32)
    state_row = packed[0:1, :] + packed[1:2, :]
    out_ref[...] = adagrad_rows(packed_ref[0:rows].astype(F32), state_row, gradient)[0]


def head_kernel(
    k, own, blocks, nat_ref, rel_ref, lo_ref, hi_ref, gu_ref, hrows_ref, table_ref, state_ref, *rest
):
    out_ref, rel_s = rest[0], rest[-1]
    rows, width = table_ref.shape
    restore_relations(nat_ref, lo_ref, hi_ref, rel_s, own)
    size = gu_ref.shape[0] // blocks
    terms = []
    for b in range(blocks):
        chosen = rel_s[pl.ds(pl.multiple_of(rel_ref[k, b] * width, width), width)]
        terms.append(dot(gu_ref[b * size : (b + 1) * size], chosen, COLS, COLS).astype(BF16))
    hot = one_hot_rows(hrows_ref[k : k + 1, :], rows)
    gradient = dot(hot, jnp.concatenate(terms), COLS, ROWS)
    table, state = adagrad_rows(table_ref[...], state_ref[...], gradient)
    out_ref[...] = table
    if len(rest) > 2:
        state_out_ref, h_ref = rest[1:3]
        state_out_ref[...] = state.T[0:1, :]
        pick = one_hot_rows(hrows_ref[k + 1 : k + 2, :], rows)
        h_ref[...] = dot(pick, table.astype(BF16), ROWS, ROWS).astype(BF16)


def call(kernel, outs, smem, scratch, flops, *args):
    outs = [jax.ShapeDtypeStruct(shape, kind) for shape, kind in outs]
    moved = sum(a.size * a.dtype.itemsize for a in (*args, *outs))
    return pl.pallas_call(
        kernel,
        out_shape=outs,
        in_specs=[SMEM] * smem + [VMEM] * (len(args) - smem),
        out_specs=[VMEM] * len(outs),
        scratch_shapes=scratch,
        compiler_params=pltpu.CompilerParams(vmem_limit_bytes=VMEM_LIMIT),
        cost_estimate=pl.CostEstimate(flops=flops, bytes_accessed=moved, transcendentals=0),
    )(*args)


class Exchange:
    def __init__(self, heads, tails):
        self.devices = heads * tails
        head_bits = [tails << i for i in range(heads.bit_length() - 1)]
        tail_bits = [1 << i for i in range(tails.bit_length() - 1)]
        rest = head_bits[1:2] + tail_bits + head_bits[2:]
        pairs = [rest[i : i + 2] for i in range(0, len(rest), 2)]
        self.stages = [head_bits[:1]] + pairs
        bits = head_bits[:1] + rest
        places = [self.others(bits, j) for j in range(self.devices)]
        slots = np.zeros(self.devices, np.int32)
        slots[places] = np.arange(self.devices)
        me = lax.axis_index(AXES)
        self.block_of_slot = jnp.asarray(places, jnp.int32) ^ me
        self.slot_of_block = jnp.asarray(slots)[jnp.arange(self.devices, dtype=jnp.int32) ^ me]

    def others(self, bits, j):
        return sum(bit for i, bit in enumerate(bits) if j >> (len(bits) - 1 - i) & 1)

    def masks(self, stage):
        return [self.others(stage, j) for j in range(1, 1 << len(stage))]

    def swap(self, x, mask):
        return lax.ppermute(x, AXES, [(i, i ^ mask) for i in range(self.devices)])

    def reduce_scatter(self, parts, hooks):
        if sum(part.shape[0] for part in parts) // self.devices % PACK_ROWS:
            both = jnp.concatenate(parts)
            both = both.reshape(self.devices, -1, both.shape[1])[self.block_of_slot]
            parts = jnp.split(both.reshape(-1, both.shape[2]), len(parts))
        if len(parts) > 2:
            half = len(parts) // 2
            mask = self.masks(self.stages[0])[0]
            got = [self.swap(part, mask) for part in parts[half:]]
            parts = [(a.astype(F32) + b.astype(F32)).astype(BF16) for a, b in zip(parts[:half], got)]
            parts[0] = hooks["own"](parts[0])
        for i, stage in enumerate(self.stages):
            if len(parts) != 1 << len(stage):
                continue
            got = [self.swap(part, mask) for part, mask in zip(parts[1:], self.masks(stage))]
            pieces = parts[:1] + hooks.get(i, list)(got)
            if i + 1 == len(self.stages):
                return sum(piece.astype(F32) for piece in pieces)
            count = 1 << len(self.stages[i + 1])
            size = pieces[0].shape[0] // count
            parts = [
                sum(piece[j * size : (j + 1) * size].astype(F32) for piece in pieces).astype(BF16)
                for j in range(count)
            ]

    def all_gather(self, own, hooks):
        rows = own.shape[0]
        for i, stage in reversed(list(enumerate(self.stages))[1:]):
            got = [self.swap(own, mask) for mask in self.masks(stage)]
            own = jnp.concatenate([own] + hooks.get(i, list)(got))
        lo, hi = own, self.swap(own, self.masks(self.stages[0])[0])
        if rows % PACK_ROWS:
            both = jnp.concatenate([lo, hi]).reshape(self.devices, rows, -1)[self.slot_of_block]
            lo, hi = jnp.split(both.reshape(self.devices * rows, -1), 2)
        return lo, hi


def shards(
    head_table,
    head_state,
    tail_table,
    tail_state,
    relations,
    relation_state,
    head_rows,
    tail_rows,
    negatives,
    relation_ids,
    block_counts,
):
    heads, tails = lax.axis_size("head"), lax.axis_size("tail")
    exchange = Exchange(heads, tails)
    nat = exchange.block_of_slot
    own = relations.shape[0]
    rows, width = tail_table.shape
    edges = head_rows.shape[1]
    blocks, nneg = negatives.shape[1:]
    all_rows = relations.shape[0] * exchange.devices
    half = all_rows // 2
    square = 2 * rows * edges * width

    head_state = head_state.reshape(1, -1)
    tail_state = tail_state.reshape(1, -1)
    held = {"indices": [head_rows, tail_rows, negatives]}

    def with_(name):
        def hook(got):
            got, held[name] = lax.optimization_barrier((got, held[name]))
            return got

        return hook

    def rotate(x):
        x = lax.ppermute(x, "tail", [(i, (i + i % 2 * 2) % tails) for i in range(tails)])
        return lax.ppermute(x, "tail", [(i, i ^ 1) for i in range(tails)])

    def prepare(got):
        held["prepared"] = call(
            prepare_kernel,
            [
                ((edges, width), BF16),
                ((rows, width), BF16),
                ((2, edges, 128), F32),
                ((2, blocks, rows), F32),
                (head_state.shape, F32),
                (tail_state.shape, F32),
            ],
            0, [], square,
            head_table, tail_table, *held["indices"], head_state, tail_state,
        )
        return with_("prepared")(got)

    gather_hooks = {2: with_("indices"), 1: prepare}
    for k in range(2):
        lo, hi = exchange.all_gather(relations.astype(BF16), gather_hooks)
        if k == 0:
            head_vecs, tail_vecs, tail_col, counts, head_state, tail_state = held["prepared"]
        else:
            tail_vecs = held["tail"]
        cuts = 2 if k == 0 else 2 << len(exchange.stages[1])
        weights, projected, edge_grad, *terms = call(
            functools.partial(score_kernel, k, own, float(nneg), cuts),
            [((edges, rows), BF16), ((edges, width), BF16), ((edges, width), BF16)]
            + [((all_rows // cuts, width), BF16)] * cuts,
            3, [pltpu.VMEM((all_rows, width), BF16), pltpu.VMEM((all_rows, width), BF16)], 5 * square,
            nat, block_counts, relation_ids, lo, hi, head_vecs, tail_vecs, tail_col, counts,
        )

        def update_heads(edge_grad, outs):
            return call(
                functools.partial(head_kernel, k, own, blocks), [(head_table.shape, F32), *outs],
                2, [pltpu.VMEM((all_rows, width), BF16)], 4 * square,
                nat, relation_ids, lo, hi, edge_grad, head_rows, head_table, head_state,
            )

        if k == 0:
            (tail_new,) = call(
                tail_kernel, [((rows + PACK_ROWS, width), BF16)], 0, [], square,
                weights, projected, tail_table, tail_state,
            )
            held["tail"] = rotate(tail_new)
            held["head"] = update_heads(edge_grad, [(head_state.shape, F32), ((edges, width), BF16)])
            grad = exchange.reduce_scatter(terms, {1: lambda got: with_("head")(got[::-1])[::-1]})
            head_table, head_state, head_vecs = held["head"]
            gather_hooks = {1: with_("tail")}
        else:

            def last_updates(part):
                part, ready = lax.optimization_barrier((part, [weights, projected, edge_grad]))
                held["tail"] = call(
                    last_tail_kernel, [((rows, width), F32)], 0, [], square, *ready[:2], tail_vecs
                )
                held["head"] = update_heads(ready[2], [])
                return part

            hooks = {"own": last_updates, 1: lambda got: with_("head")(got[::-1])[::-1], 2: with_("tail")}
            grad = exchange.reduce_scatter(terms, hooks)
        relation_state = relation_state + grad * grad
        relations = relations - RATE_RELATIONS * grad / (jnp.sqrt(relation_state) + EPSILON)
    return (held["head"][0], held["tail"][0], relations)


def solution(mesh):
    both = P(AXES, None)
    in_specs = (
        both,
        P(AXES),
        both,
        P(AXES),
        both,
        both,
        P(None, AXES),
        P(None, AXES),
        P(None, AXES, None),
        P(None, AXES),
        P(None, AXES),
    )
    return jax.shard_map(
        shards, mesh=mesh, in_specs=in_specs, out_specs=(both, both, both), check_vma=False
    )
```

```python
import functools

import jax
import jax.numpy as jnp
import numpy as np
from jax import lax
from jax.experimental import pallas as pl
from jax.experimental.pallas import tpu as pltpu
from jax.sharding import PartitionSpec as P

RATE_ROWS = 0.2
RATE_RELATIONS = 0.05
EPSILON = 1e-06
AXES = ("head", "tail")
F32, BF16 = jnp.float32, jnp.bfloat16
ROWS, COLS = 0, 1
PACK_ROWS = 16
VMEM_LIMIT = 24 * 1024 * 1024
VMEM = pl.BlockSpec(memory_space=pltpu.VMEM)
SMEM = pl.BlockSpec(memory_space=pltpu.SMEM)


def dot(a, b, contract_a, contract_b):
    return lax.dot_general(
        a, b, (((contract_a,), (contract_b,)), ((), ())), preferred_element_type=F32
    )


def to_column(row):
    return jnp.broadcast_to(row, (128, row.shape[1])).T


def spread(column, width):
    return jnp.concatenate([column] * (width // column.shape[1]), axis=1)


def adagrad_rows(table, state_row, gradient):
    width = gradient.shape[1]
    mean = jnp.sum(gradient * gradient, axis=1, keepdims=True) * (1.0 / width)
    state = to_column(state_row) + mean
    factor = RATE_ROWS / (jnp.sqrt(state) + EPSILON)
    return table - gradient * spread(factor, width), state


def one_hot_rows(index_row, rows):
    n = index_row.shape[1]
    return (lax.broadcasted_iota(jnp.int32, (rows, n), 0) == index_row).astype(F32).astype(BF16)


def restore_relations(nat_ref, lo_ref, hi_ref, rel_s, own):
    half = lo_ref.shape[0]
    if own % PACK_ROWS:
        rel_s[:half] = lo_ref[...]
        rel_s[half:] = hi_ref[...]
        return
    for part, ref in enumerate((lo_ref, hi_ref)):
        for j in range(half // own):
            block = nat_ref[part * (half // own) + j]
            rel_s[pl.ds(pl.multiple_of(block * own, own), own)] = ref[j * own : (j + 1) * own]


def prepare_kernel(
    head_ref, tail_ref, hrows_ref, trows_ref, neg_ref, hstate_ref, tstate_ref,
    h_ref, t_ref, tcol_ref, cnt_ref, hstate_out_ref, tstate_out_ref,
):
    hstate_out_ref[...] = hstate_ref[...]
    tstate_out_ref[...] = tstate_ref[...]
    buckets = hrows_ref.shape[0]
    blocks, nneg = neg_ref.shape[1:]
    pick = one_hot_rows(hrows_ref[0:1, :], head_ref.shape[0])
    h_ref[...] = dot(pick, head_ref[...].astype(BF16), ROWS, ROWS).astype(BF16)
    t_ref[...] = tail_ref[...].astype(BF16)
    ones = jnp.ones((8, nneg), BF16)
    for k in range(buckets):
        tcol_ref[k] = to_column(trows_ref[k : k + 1, :].astype(F32))
        for b in range(blocks):
            hot = one_hot_rows(neg_ref[k, b : b + 1, :], tail_ref.shape[0])
            cnt_ref[k, b : b + 1, :] = dot(ones, hot, COLS, COLS)[0:1, :]


def score_kernel(
    k, own, nneg, cuts, nat_ref, live_ref, rel_ref, lo_ref, hi_ref, h_ref, t_ref, tcol_ref, cnt_ref,
    w_ref, u_ref, gu_ref, *rest,
):
    grad_refs, (rel_s, grad_s) = rest[:cuts], rest[cuts:]
    edges, width = h_ref.shape
    blocks, rows = cnt_ref.shape[1:]
    size = edges // blocks
    relations = rel_s.shape[0] // width
    restore_relations(nat_ref, lo_ref, hi_ref, rel_s, own)
    for b in range(blocks):
        part = slice(b * size, (b + 1) * size)
        chosen = rel_s[pl.ds(pl.multiple_of(rel_ref[k, b] * width, width), width)]
        u_ref[part] = dot(h_ref[part], chosen, COLS, ROWS).astype(BF16)
    tails = t_ref[0:rows]
    score = dot(u_ref[...], tails, COLS, COLS)
    row_id = lax.broadcasted_iota(jnp.int32, (size, rows), 1).astype(F32)
    for b in range(blocks):
        part = slice(b * size, (b + 1) * size)
        half_live = jnp.where(live_ref[k, 0] > b, 0.5, 0.0)
        share = cnt_ref[k, b : b + 1, :] * (half_live / nneg)
        t = jnp.tanh(0.5 * score[part])
        is_tail = spread(tcol_ref[k, part], rows) == row_id
        weight = (share + share * t) - jnp.where(is_tail, half_live - half_live * t, 0.0)
        w_ref[part] = weight.astype(BF16)
    gu = dot(w_ref[...], tails, COLS, ROWS).astype(BF16)
    gu_ref[...] = gu
    for r in range(relations):
        parts = []
        for b in range(blocks):
            part = h_ref[b * size : (b + 1) * size]
            parts.append(jnp.where(rel_ref[k, b] == r, part, jnp.zeros_like(part)))
        grad_s[r * width : (r + 1) * width] = dot(jnp.concatenate(parts), gu, ROWS, ROWS).astype(BF16)
    for i, ref in enumerate(grad_refs):
        count = ref.shape[0]
        if own % PACK_ROWS:
            ref[...] = grad_s[i * count : (i + 1) * count]
            continue
        for j in range(count // own):
            block = nat_ref[i * (count // own) + j]
            ref[j * own : (j + 1) * own] = grad_s[pl.ds(pl.multiple_of(block * own, own), own)]


def tail_kernel(w_ref, u_ref, table_ref, state_ref, out_ref):
    rows, width = table_ref.shape
    gradient = dot(w_ref[...], u_ref[...], ROWS, ROWS)
    table, state = adagrad_rows(table_ref[...], state_ref[...], gradient)
    out_ref[0:rows] = table.astype(BF16)
    state_row = state.T[0:1, :]
    high = state_row.astype(BF16).astype(F32)
    row_id = lax.broadcasted_iota(jnp.int32, (PACK_ROWS, width), 0)
    packed = jnp.where(row_id == 0, high, jnp.where(row_id == 1, state_row - high, 0.0))
    out_ref[rows : rows + PACK_ROWS] = packed.astype(BF16)


def last_tail_kernel(w_ref, u_ref, packed_ref, out_ref):
    rows = out_ref.shape[0]
    gradient = dot(w_ref[...], u_ref[...], ROWS, ROWS)
    packed = packed_ref[rows : rows + PACK_ROWS].astype(F32)
    state_row = packed[0:1, :] + packed[1:2, :]
    out_ref[...] = adagrad_rows(packed_ref[0:rows].astype(F32), state_row, gradient)[0]


def head_kernel(
    k, own, blocks, nat_ref, rel_ref, lo_ref, hi_ref, gu_ref, hrows_ref, table_ref, state_ref, *rest
):
    out_ref, rel_s = rest[0], rest[-1]
    rows, width = table_ref.shape
    restore_relations(nat_ref, lo_ref, hi_ref, rel_s, own)
    size = gu_ref.shape[0] // blocks
    terms = []
    for b in range(blocks):
        chosen = rel_s[pl.ds(pl.multiple_of(rel_ref[k, b] * width, width), width)]
        terms.append(dot(gu_ref[b * size : (b + 1) * size], chosen, COLS, COLS).astype(BF16))
    hot = one_hot_rows(hrows_ref[k : k + 1, :], rows)
    gradient = dot(hot, jnp.concatenate(terms), COLS, ROWS)
    table, state = adagrad_rows(table_ref[...], state_ref[...], gradient)
    out_ref[...] = table
    if len(rest) > 2:
        state_out_ref, h_ref = rest[1:3]
        state_out_ref[...] = state.T[0:1, :]
        pick = one_hot_rows(hrows_ref[k + 1 : k + 2, :], rows)
        h_ref[...] = dot(pick, table.astype(BF16), ROWS, ROWS).astype(BF16)


def call(kernel, outs, smem, scratch, flops, *args):
    outs = [jax.ShapeDtypeStruct(shape, kind) for shape, kind in outs]
    moved = sum(a.size * a.dtype.itemsize for a in (*args, *outs))
    return pl.pallas_call(
        kernel,
        out_shape=outs,
        in_specs=[SMEM] * smem + [VMEM] * (len(args) - smem),
        out_specs=[VMEM] * len(outs),
        scratch_shapes=scratch,
        compiler_params=pltpu.CompilerParams(vmem_limit_bytes=VMEM_LIMIT),
        cost_estimate=pl.CostEstimate(flops=flops, bytes_accessed=moved, transcendentals=0),
    )(*args)


class Exchange:
    def __init__(self, heads, tails):
        self.devices = heads * tails
        head_bits = [tails << i for i in range(heads.bit_length() - 1)]
        tail_bits = [1 << i for i in range(tails.bit_length() - 1)]
        rest = head_bits[1:2] + tail_bits + head_bits[2:]
        pairs = [rest[i : i + 2] for i in range(0, len(rest), 2)]
        self.stages = [head_bits[:1]] + pairs
        bits = head_bits[:1] + rest
        places = [self.others(bits, j) for j in range(self.devices)]
        slots = np.zeros(self.devices, np.int32)
        slots[places] = np.arange(self.devices)
        me = lax.axis_index(AXES)
        self.block_of_slot = jnp.asarray(places, jnp.int32) ^ me
        self.slot_of_block = jnp.asarray(slots)[jnp.arange(self.devices, dtype=jnp.int32) ^ me]

    def others(self, bits, j):
        return sum(bit for i, bit in enumerate(bits) if j >> (len(bits) - 1 - i) & 1)

    def masks(self, stage):
        return [self.others(stage, j) for j in range(1, 1 << len(stage))]

    def swap(self, x, mask):
        return lax.ppermute(x, AXES, [(i, i ^ mask) for i in range(self.devices)])

    def reduce_scatter(self, parts, hooks):
        if sum(part.shape[0] for part in parts) // self.devices % PACK_ROWS:
            both = jnp.concatenate(parts)
            both = both.reshape(self.devices, -1, both.shape[1])[self.block_of_slot]
            parts = jnp.split(both.reshape(-1, both.shape[2]), len(parts))
        if len(parts) > 2:
            half = len(parts) // 2
            mask = self.masks(self.stages[0])[0]
            got = [self.swap(part, mask) for part in parts[half:]]
            parts = [(a.astype(F32) + b.astype(F32)).astype(BF16) for a, b in zip(parts[:half], got)]
            parts[0] = hooks["own"](parts[0])
        for i, stage in enumerate(self.stages):
            if len(parts) != 1 << len(stage):
                continue
            got = [self.swap(part, mask) for part, mask in zip(parts[1:], self.masks(stage))]
            pieces = parts[:1] + hooks.get(i, list)(got)
            if i + 1 == len(self.stages):
                return sum(piece.astype(F32) for piece in pieces)
            count = 1 << len(self.stages[i + 1])
            size = pieces[0].shape[0] // count
            parts = [
                sum(piece[j * size : (j + 1) * size].astype(F32) for piece in pieces).astype(BF16)
                for j in range(count)
            ]

    def all_gather(self, own, hooks):
        rows = own.shape[0]
        for i, stage in reversed(list(enumerate(self.stages))[1:]):
            got = [self.swap(own, mask) for mask in self.masks(stage)]
            own = jnp.concatenate([own] + hooks.get(i, list)(got))
        lo, hi = own, self.swap(own, self.masks(self.stages[0])[0])
        if rows % PACK_ROWS:
            both = jnp.concatenate([lo, hi]).reshape(self.devices, rows, -1)[self.slot_of_block]
            lo, hi = jnp.split(both.reshape(self.devices * rows, -1), 2)
        return lo, hi


def shards(
    head_table,
    head_state,
    tail_table,
    tail_state,
    relations,
    relation_state,
    head_rows,
    tail_rows,
    negatives,
    relation_ids,
    block_counts,
):
    heads, tails = lax.axis_size("head"), lax.axis_size("tail")
    exchange = Exchange(heads, tails)
    nat = exchange.block_of_slot
    own = relations.shape[0]
    rows, width = tail_table.shape
    edges = head_rows.shape[1]
    blocks, nneg = negatives.shape[1:]
    all_rows = relations.shape[0] * exchange.devices
    half = all_rows // 2
    square = 2 * rows * edges * width

    head_state = head_state.reshape(1, -1)
    tail_state = tail_state.reshape(1, -1)
    held = {"indices": [head_rows, tail_rows, negatives]}

    def with_(name):
        def hook(got):
            got, held[name] = lax.optimization_barrier((got, held[name]))
            return got

        return hook

    def rotate(x):
        x = lax.ppermute(x, "tail", [(i, (i + i % 2 * 2) % tails) for i in range(tails)])
        return lax.ppermute(x, "tail", [(i, i ^ 1) for i in range(tails)])

    def prepare(got):
        held["prepared"] = call(
            prepare_kernel,
            [
                ((edges, width), BF16),
                ((rows, width), BF16),
                ((2, edges, 128), F32),
                ((2, blocks, rows), F32),
                (head_state.shape, F32),
                (tail_state.shape, F32),
            ],
            0, [], square,
            head_table, tail_table, *held["indices"], head_state, tail_state,
        )
        return with_("prepared")(got[::-1])[::-1]

    gather_hooks = {2: with_("indices"), 1: prepare}
    for k in range(2):
        lo, hi = exchange.all_gather(relations.astype(BF16), gather_hooks)
        if k == 0:
            head_vecs, tail_vecs, tail_col, counts, head_state, tail_state = held["prepared"]
        else:
            tail_vecs = held["tail"]
        cuts = 2 if k == 0 else 2 << len(exchange.stages[1])
        weights, projected, edge_grad, *terms = call(
            functools.partial(score_kernel, k, own, float(nneg), cuts),
            [((edges, rows), BF16), ((edges, width), BF16), ((edges, width), BF16)]
            + [((all_rows // cuts, width), BF16)] * cuts,
            3, [pltpu.VMEM((all_rows, width), BF16), pltpu.VMEM((all_rows, width), BF16)], 5 * square,
            nat, block_counts, relation_ids, lo, hi, head_vecs, tail_vecs, tail_col, counts,
        )

        def update_heads(edge_grad, outs):
            return call(
                functools.partial(head_kernel, k, own, blocks), [(head_table.shape, F32), *outs],
                2, [pltpu.VMEM((all_rows, width), BF16)], 4 * square,
                nat, relation_ids, lo, hi, edge_grad, head_rows, head_table, head_state,
            )

        if k == 0:
            (tail_new,) = call(
                tail_kernel, [((rows + PACK_ROWS, width), BF16)], 0, [], square,
                weights, projected, tail_table, tail_state,
            )
            held["tail"] = rotate(tail_new)
            held["head"] = update_heads(edge_grad, [(head_state.shape, F32), ((edges, width), BF16)])
            grad = exchange.reduce_scatter(terms, {1: lambda got: with_("head")(got[::-1])[::-1]})
            head_table, head_state, head_vecs = held["head"]
            gather_hooks = {1: with_("tail")}
        else:

            def last_updates(part):
                part, ready = lax.optimization_barrier((part, [weights, projected, edge_grad]))
                held["tail"] = call(
                    last_tail_kernel, [((rows, width), F32)], 0, [], square, *ready[:2], tail_vecs
                )
                held["head"] = update_heads(ready[2], [])
                return part

            hooks = {"own": last_updates, 1: lambda got: with_("head")(got[::-1])[::-1], 2: with_("tail")}
            grad = exchange.reduce_scatter(terms, hooks)
        relation_state = relation_state + grad * grad
        relations = relations - RATE_RELATIONS * grad / (jnp.sqrt(relation_state) + EPSILON)
    return (held["head"][0], held["tail"][0], relations)


def solution(mesh):
    both = P(AXES, None)
    in_specs = (
        both,
        P(AXES),
        both,
        P(AXES),
        both,
        both,
        P(None, AXES),
        P(None, AXES),
        P(None, AXES, None),
        P(None, AXES),
        P(None, AXES),
    )
    return jax.shard_map(
        shards, mesh=mesh, in_specs=in_specs, out_specs=(both, both, both), check_vma=False
    )
```
